32 devices in a mesh: seq: 8 (over z, x), head: 4 (over y, core).
Axes of the slice: x: 2, y: 2, z: 4, core: 2. Of those that a mesh axis runs over, the one named last changes fastest.
Arguments:
- tokens: bfloat16 [2048, 3072], P('seq'), may hold values from -16 to 16
- qkv_weight: bfloat16 [3072, 3, 1536], P(None, None, 'head'), may hold values from -1 to 1
- q_gain: float32 [128], replicated, may hold values from 0.5 to 6
- k_gain: float32 [128], replicated, may hold values from 0.5 to 6
- out_weight: bfloat16 [1536, 3072], P('head'), may hold values from -0.15625 to 0.15625
- query_cluster: int32 [12, 2048, 1], P('head', 'seq'), may hold values from 0 to 7; in each aligned block of 256 rows (0 to 255, 256 to 511, ..., all dimensions but the last counted through in order) at most 40 rows name the same one
- key_cluster: int32 [12, 2048, 1], P('head', 'seq'), may hold values from 0 to 31, as said below
- query_slot: int32 [12, 8], P('head'), may hold values from 0 to 7, each once within a row
- key_slot: int32 [12, 32], P('head'), may hold values from 0 to 31, as said below
- pairs: int32 [12, 8, 8], P('head'), may hold values from 0 to 31, as said below
Outputs:
- attention_out: bfloat16 [2048, 3072], P('seq', 'head')
The draws below stay inside these ranges and needn't reach their ends.
Inputs may be any that keep to these rules, and one draw needn't show every extreme that they name: `query_cluster`: counting the tokens of one device, each query cluster is named at most 40 times in each head. `key_cluster`: in each head, the tokens of one device name 16 key clusters exactly 16 times each and no other; every key cluster is named by exactly 64 tokens in all. Each row is a permutation; query cluster c of head h is owned by index query_slot[h, c] of seq. Each row is a permutation; key cluster c of head h is owned by index key_slot[h, c] // 4 of seq. `pairs`: each list holds 8 key owner slots, exactly one from each range of 4 slots that one index of seq owns, in no particular order.
All inputs are finite; a program needn't handle non-finite values.
Results may differ from the reference program's by a relative error of at most 0.012.
The reference program's roundings to bfloat16 on the way count: a program that leaves them out, or rounds other values in their place, can miss the bound.
Values may be sent and summed in bfloat16 or wider, within the bound.
A program may use at most 128 MiB of HBM per device.

```python
import math
import jax
import jax.numpy as jnp
import numpy as np
from jax import lax

D = 3072
HD = 128
HEADS = 12
TOK_DEV = 256
KCL_DEV = 4
TOKENS = 2048
QCL = 8
KCL = 32
MOSTQ = 40
MOSTK = 16
QROWS = 320
KROWS = 128


def key_order(key):
    streams = jax.random.split(key, HEADS)
    return jax.vmap(lambda stream: jax.random.permutation(stream, KCL))(streams).astype(jnp.int32)


def row_scales(key, rows, lowest, highest):
    return jnp.exp(jax.random.uniform(key, (rows, 1), jnp.float32, math.log(lowest), math.log(highest)))


def draw_tokens(key, part):
    key = jax.random.fold_in(key, 11)
    key_base, key_scale = jax.random.split(key, 2)
    scales = row_scales(key_scale, TOKENS, 0.4, 4.0)
    drawn = jax.random.truncated_normal(key_base, -4.0, 4.0, (TOKENS, D), jnp.float32)
    return (drawn * scales).astype(jnp.bfloat16)


def draw_qkv_weight(key, part):
    key = jax.random.fold_in(key, 12)
    root_size = math.sqrt(D)
    drawn = jax.random.truncated_normal(key, -4.0, 4.0, (D, 3, HEADS * HD), jnp.float32) / root_size
    return drawn.astype(jnp.bfloat16)


def draw_q_gain(key, part):
    key = jax.random.fold_in(key, 13)
    return jax.random.uniform(key, (HD,), jnp.float32, 0.5, 1.5)


def draw_k_gain(key, part):
    key = jax.random.fold_in(key, 14)
    return jax.random.uniform(key, (HD,), jnp.float32, 0.5, 1.5)


def draw_key_cluster(key, part):
    key = jax.random.fold_in(key, 15)
    key_rank, key_place = jax.random.split(key)
    members = TOKENS // TOK_DEV
    used = TOK_DEV // MOSTK
    rank_streams = jax.random.split(key_rank, HEADS)
    ranking = jax.vmap(lambda stream: jax.random.permutation(stream, KCL))(rank_streams).astype(jnp.int32)
    devices = jnp.arange(members, dtype=jnp.int32)[:, None]
    within = jnp.arange(TOK_DEV, dtype=jnp.int32)[None, :]
    ranks = (devices * used + within // MOSTK) % KCL
    labels = jnp.take(ranking, ranks.reshape(-1), axis=1).reshape(HEADS, members, TOK_DEV)
    place_streams = jax.random.split(key_place, HEADS * members)
    shuffles = jax.vmap(lambda stream: jax.random.permutation(stream, TOK_DEV))(place_streams)
    shuffles = shuffles.reshape(HEADS, members, TOK_DEV).astype(jnp.int32)
    mixed = jnp.take_along_axis(labels, shuffles, axis=2)
    return mixed.reshape(HEADS, TOKENS, 1).astype(jnp.int32)


def draw_key_slot(key, part):
    return key_order(jax.random.fold_in(key, 16))


def draw_pairs(key, part):
    key = jax.random.fold_in(key, 21)
    key_local, key_shuffle = jax.random.split(key)
    local_pick = jax.random.randint(key_local, (HEADS, QCL, QCL), 0, KCL_DEV).astype(jnp.int32)
    owners = jnp.arange(QCL, dtype=jnp.int32)[None, None, :]
    wanted_slot = owners * KCL_DEV + local_pick
    list_keys = jax.random.split(key_shuffle, HEADS * QCL)
    shuffles = jax.vmap(lambda stream: jax.random.permutation(stream, QCL))(list_keys)
    shuffles = shuffles.reshape(HEADS, QCL, QCL).astype(jnp.int32)
    return jnp.take_along_axis(wanted_slot, shuffles, axis=2).astype(jnp.int32)


def level_of(stream_key, dims, pieces, low, largest):
    factor_of = 1.0
    for position, parts in pieces:
        heights = jax.random.uniform(jax.random.fold_in(jax.random.fold_in(stream_key, 6), position), (parts,), jnp.float32, low / len(pieces), largest / len(pieces))
        factor_of = factor_of * jnp.repeat(jnp.exp(heights), dims[position] // parts).reshape((-1,) + (1,) * (len(dims) - 1 - position))
    return factor_of


def assign_block(own_key, own, number, rows, amount, top, bound, slope):
    sequence = jax.random.permutation(own_key, amount)
    crowded, usual = load_shares(amount, rows * top, bound, slope, True), load_shares(amount, rows * top, bound, slope, False)
    places = jnp.arange(amount)

    def named(tallies, rotation):
        used = int((tallies > 0).sum())
        fixed = max(1, used // 4)
        moved = fixed + (places - fixed + rotation * (used - fixed)) % max(1, amount - fixed)
        return jnp.zeros((amount,), jnp.int32).at[sequence[jnp.where(places < fixed, places, moved)]].set(jnp.asarray(tallies, jnp.int32))

    tallies = jnp.where(number % 4 == 0, named(crowded, number // 4), named(usual, number - number // 4 - 1))
    mixed = jax.random.permutation(jax.random.fold_in(own, 3), amount)
    donor, sink = mixed[0:amount // 2 * 2:2], mixed[1:amount // 2 * 2:2]
    slack = jnp.minimum(tallies[donor] - 1, bound - tallies[sink]) // 2
    slack = jnp.where((donor == sequence[0]) | (sink == sequence[0]) | (tallies[sink] == 0), 0, jnp.maximum(slack, 0))
    moved = jax.random.randint(jax.random.fold_in(own, 4), (amount // 2,), 0, 1 << 20) % (slack + 1)
    tallies = tallies.at[donor].add(-moved).at[sink].add(moved)
    items = jnp.searchsorted(jnp.cumsum(tallies), jnp.arange(rows * top), side="right").astype(jnp.int32)
    grid = items.reshape(top, rows).T
    grid = grid[jax.random.permutation(jax.random.fold_in(own, 1), rows)]
    rotation = jax.random.randint(jax.random.fold_in(own, 2), (rows, 1), 0, top)
    return jnp.take_along_axis(grid, (jnp.arange(top)[None, :] + rotation) % top, axis=1)


def load_shares(count, total, bound, lean, full):
    weights = [(1 << 20) // math.isqrt(grade ** lean) + 1 for grade in range(1, count + 1)]
    largest = bound if full else min(bound, max(-(-total // count), total * weights[0] // sum(weights)))
    least = 1 if total - largest >= count - 1 else 0
    holding, surplus = [largest] + [least] * (count - 1), total - largest - least * (count - 1)
    while surplus > 0:
        movable = [i for i in range(1, count) if holding[i] < largest] or [i for i in range(1, count) if holding[i] < bound]
        whole, budget = sum([weights[i] for i in movable]), surplus
        for i in movable:
            addition = min(bound - holding[i], max(1, budget * weights[i] // whole), surplus)
            holding[i] = holding[i] + addition
            surplus = surplus - addition
    return np.array(holding)


def scatter_about(key, dims, deviation, reach, cuts=(), kind=jnp.bfloat16):
    entries = jax.random.normal(key, dims, jnp.float32) * deviation
    if len(cuts) > 0:
        entries = level_of(key, dims, cuts, -0.22, 0.18) * entries
    return jnp.clip(entries, min=-reach, max=reach).astype(kind)


def setup_inputs(seed: int = 0) -> dict:
    seeds = jax.random.split(jax.random.key(seed), 11)
    tokens = draw_tokens(jax.random.fold_in(seeds[10], 71), 0)
    qkv_weight = draw_qkv_weight(jax.random.fold_in(seeds[10], 71), 0)
    q_gain = draw_q_gain(jax.random.fold_in(seeds[10], 71), 0)
    k_gain = draw_k_gain(jax.random.fold_in(seeds[10], 71), 0)
    out_weight = scatter_about(seeds[4], (HEADS * HD, D), (HEADS * HD) ** -0.5, 0.15625, ((0, 4),))
    query_cluster_keys = jax.random.split(jax.random.fold_in(seeds[5], 1), HEADS * TOKENS // TOK_DEV)
    query_cluster_turns = jax.random.permutation(jax.random.fold_in(seeds[5], 3), HEADS * TOKENS // TOK_DEV)
    query_cluster = jax.vmap(lambda own, number: assign_block(jax.random.fold_in(seeds[5], 2), own, number, TOK_DEV, QCL, 1, MOSTQ, 1))(query_cluster_keys, query_cluster_turns).reshape((HEADS, TOKENS, 1))
    key_cluster = draw_key_cluster(jax.random.fold_in(seeds[10], 71), 0)
    query_slot = jax.vmap(lambda own: jax.random.permutation(own, QCL))(jax.random.split(seeds[7], HEADS)).reshape((HEADS, QCL)).astype(jnp.int32)
    key_slot = draw_key_slot(jax.random.fold_in(seeds[10], 71), 0)
    pairs = draw_pairs(jax.random.fold_in(seeds[10], 71), 0)
    return {"tokens": tokens, "qkv_weight": qkv_weight, "q_gain": q_gain, "k_gain": k_gain, "out_weight": out_weight, "query_cluster": query_cluster, "key_cluster": key_cluster, "query_slot": query_slot, "key_slot": key_slot, "pairs": pairs}


EPSILON = 1e-06

def normalize(projected, gain):
    mean_square = lax.optimization_barrier(jnp.mean(projected * projected, axis=-1, keepdims=True))
    return projected * lax.rsqrt(mean_square + EPSILON) * gain

def cluster_table(labels, clusters, depth):
    order = jnp.argsort(labels).astype(jnp.int32)
    counts = jnp.bincount(labels, length=clusters).astype(jnp.int32)
    starts = (jnp.cumsum(counts) - counts).astype(jnp.int32)
    offsets = jnp.arange(depth, dtype=jnp.int32)
    places = starts[:, None] + offsets[None, :]
    present = offsets[None, :] < counts[:, None]
    picked = order[jnp.clip(places, 0, labels.shape[0] - 1)]
    return (jnp.where(present, picked, 0).astype(jnp.int32), present)

def attend_block(query_block, key_block, value_block, usable):
    inverse_root = 1.0 / math.sqrt(HD)
    scores = lax.dot_general(query_block, key_block, (((1,), (1,)), ((), ())), preferred_element_type=jnp.float32) * inverse_root
    allowed = usable[None, :]
    highest = lax.optimization_barrier(jnp.max(jnp.where(allowed, scores, -1e+30), axis=1, keepdims=True))
    weights = jnp.where(allowed, jnp.exp(jnp.where(allowed, scores, highest) - highest), 0.0)
    denominator = jnp.maximum(lax.optimization_barrier(jnp.sum(weights, axis=1, keepdims=True)), 1.0)
    summed = jnp.dot(weights.astype(jnp.bfloat16), value_block, preferred_element_type=jnp.float32)
    return (summed / denominator).astype(jnp.bfloat16)

def reference(tokens, qkv_weight, q_gain, k_gain, out_weight, query_cluster, key_cluster, query_slot, key_slot, pairs):

    def one_head(head_index):
        head_index = head_index.astype(jnp.int32)
        weight = lax.dynamic_slice_in_dim(qkv_weight, head_index * HD, HD, 2).reshape(D, 3 * HD)
        projected = jnp.dot(tokens, weight, preferred_element_type=jnp.float32).reshape(TOKENS, 3, HD)
        queries = normalize(projected[:, 0], q_gain).astype(jnp.bfloat16)
        keys = normalize(projected[:, 1], k_gain).astype(jnp.bfloat16)
        values = projected[:, 2].astype(jnp.bfloat16)
        query_table, query_present = cluster_table(query_cluster[head_index, :, 0], QCL, QROWS)
        key_table, key_present = cluster_table(key_cluster[head_index, :, 0], KCL, KROWS)
        cluster_of_slot = jnp.argsort(key_slot[head_index]).astype(jnp.int32)

        def one_cluster(cluster_index):
            cluster_index = cluster_index.astype(jnp.int32)
            listed = cluster_of_slot[pairs[head_index, query_slot[head_index, cluster_index]]]
            query_rows = queries[query_table[cluster_index]]
            key_index = key_table[listed].reshape(-1)
            usable = key_present[listed].reshape(-1)
            return attend_block(query_rows, keys[key_index], values[key_index], usable)
        blocks = lax.map(one_cluster, jnp.arange(QCL, dtype=jnp.int32))
        target = jnp.where(query_present, query_table, TOKENS).reshape(-1)
        result = jnp.zeros((TOKENS, HD), jnp.bfloat16)
        return result.at[target].set(blocks.reshape(-1, HD), mode='drop')
    heads_out = lax.map(one_head, jnp.arange(HEADS, dtype=jnp.int32))
    joined = heads_out.transpose(1, 0, 2).reshape(TOKENS, HEADS * HD)
    return jnp.dot(joined, out_weight, preferred_element_type=jnp.float32).astype(jnp.bfloat16)
```

```python
import functools
import math

import jax
import jax.numpy as jnp
from jax import lax
from jax.experimental import pallas as pl
from jax.experimental.pallas import tpu as pltpu
from jax.sharding import PartitionSpec as P

EPSILON = 1e-06
NEG = -2e30
START = -1e30
MESH = pl.DeviceIdType.MESH
LANES = 128
INFO = 16


def normalize(projected, gain):
    mean_square = jnp.mean(projected * projected, axis=-1, keepdims=True)
    return projected * lax.rsqrt(mean_square + EPSILON) * gain


def ring_index(position, n):
    return jnp.where(position < n // 2, 2 * position, 2 * (n - 1 - position) + 1)


def kernel(
    n, groups, tok_ref, wqkv_ref, qg_ref, kg_ref, wout_ref, neg_ref, info_ref, out_ref,
    tok_v, w_v, kv, q_v, m_s, l_s, acc_s, att, wall,
    load_sem, right_send, right_recv, left_send, left_recv,
    att_send, att_recv, wt_send, wt_recv,
):
    heads, rows, width = q_v.shape
    cols = out_ref.shape[1]
    half = n // 2
    seq = lax.axis_index("seq")
    mine = lax.axis_index("head")
    pos = jnp.where(seq % 2 == 0, seq // 2, n - 1 - seq // 2)
    right = ring_index((pos + 1) % n, n)
    left = ring_index((pos + n - 1) % n, n)

    tok_load = pltpu.make_async_copy(tok_ref, tok_v, load_sem.at[0])
    tok_load.start()
    w_loads = [pltpu.make_async_copy(wqkv_ref.at[j], w_v.at[j], load_sem.at[1 + j]) for j in range(3)]
    for j in (1, 2, 0):
        w_loads[j].start()
    own_cols = pl.ds(pl.multiple_of(mine * cols, LANES), cols)
    own_load = pltpu.make_async_copy(wout_ref.at[:, :, own_cols], wall.at[:, mine], load_sem.at[4])
    own_load.start()

    barrier = pltpu.get_barrier_semaphore()
    for neighbour in (left, right):
        pl.semaphore_signal(barrier, inc=1, device_id={"seq": neighbour}, device_id_type=MESH)
    for offset in range(1, groups):
        pl.semaphore_signal(
            barrier, inc=1, device_id={"head": (mine + offset) % groups}, device_id_type=MESH
        )

    def rightward(slot, h, hop, low, size):
        part = kv.at[slot, h, pl.ds(low, size)]
        return pltpu.make_async_remote_copy(
            src_ref=part, dst_ref=part, send_sem=right_send.at[hop, h],
            recv_sem=right_recv.at[hop, h], device_id={"seq": right}, device_id_type=MESH,
        )

    def leftward(slot, h, hop, low, size):
        part = kv.at[slot, h, pl.ds(low, size)]
        return pltpu.make_async_remote_copy(
            src_ref=part, dst_ref=part, send_sem=left_send.at[hop, h],
            recv_sem=left_recv.at[hop, h], device_id={"seq": left}, device_id_type=MESH,
        )

    full = (0, 2 * rows + INFO)
    key_part = (rows, rows + INFO)
    value_part = (0, rows)

    def weights_copy(offset):
        peer = (mine + offset) % groups
        peer_cols = pl.ds(pl.multiple_of(peer * cols, LANES), cols)
        return pltpu.make_async_remote_copy(
            src_ref=wout_ref.at[:, :, peer_cols], dst_ref=wall.at[:, mine],
            send_sem=wt_send.at[offset], recv_sem=wt_recv.at[offset],
            device_id={"head": peer}, device_id_type=MESH,
        )

    def att_copy(offset, h):
        peer = (mine + offset) % groups
        return pltpu.make_async_remote_copy(
            src_ref=att.at[h, mine], dst_ref=att.at[h, mine],
            send_sem=att_send.at[offset, h], recv_sem=att_recv.at[offset, h],
            device_id={"head": peer}, device_id_type=MESH,
        )

    tok_load.wait()
    w_loads[1].wait()
    keys = jnp.dot(tok_v[...], w_v[1], preferred_element_type=jnp.float32)
    for h in range(heads):
        kv[pos, h, pl.ds(rows, rows)] = normalize(
            keys[:, h * width : (h + 1) * width], kg_ref[...]
        ).astype(jnp.bfloat16)
        kv[pos, h, pl.ds(2 * rows, INFO)] = info_ref[h]
    w_loads[2].wait()
    values = jnp.dot(tok_v[...], w_v[2], preferred_element_type=jnp.float32)
    for h in range(heads):
        kv[pos, h, pl.ds(0, rows)] = values[:, h * width : (h + 1) * width].astype(jnp.bfloat16)

    pl.semaphore_wait(barrier, 1 + groups)
    for h in range(heads):
        rightward(pos, h, 0, *full).start()
        leftward(pos, h, 0, *full).start()
    for offset in range(1, groups):
        weights_copy(offset).start()

    w_loads[0].wait()
    queries = jnp.dot(tok_v[...], w_v[0], preferred_element_type=jnp.float32)
    for h in range(heads):
        q_v[h] = normalize(queries[:, h * width : (h + 1) * width], qg_ref[...]).astype(
            jnp.bfloat16
        )
    m_s[...] = jnp.full(m_s.shape, START, jnp.float32)
    l_s[...] = jnp.zeros(l_s.shape, jnp.float32)
    acc_s[...] = jnp.zeros(acc_s.shape, jnp.float32)
    factor = math.log2(math.e) / math.sqrt(width)

    def attend(slot, h):
        block_values = kv[slot, h, pl.ds(0, rows)]
        block_keys = kv[slot, h, pl.ds(rows, rows)]
        info = kv[slot, h, pl.ds(2 * rows, INFO)].astype(jnp.float32)
        row = jnp.concatenate([info[r : r + 1, :] for r in range(rows // LANES)], axis=1)
        slots = neg_ref.shape[2]
        ids = lax.broadcasted_iota(jnp.int32, (slots, rows), 0).astype(jnp.float32)
        owner = jnp.where(ids == row, 1.0, 0.0).astype(jnp.bfloat16)
        scores = lax.dot_general(
            q_v[h], block_keys, (((1,), (1,)), ((), ())), preferred_element_type=jnp.float32
        ) + jnp.dot(neg_ref[h], owner, preferred_element_type=jnp.float32)
        before = m_s[h][:, :1]
        highest = jnp.maximum(before, jnp.max(scores, axis=1, keepdims=True))
        weights = jnp.exp2((scores - highest) * factor)
        shrink = jnp.exp2((before - highest) * factor)
        total = l_s[h][:, :1] * shrink + jnp.sum(weights, axis=1, keepdims=True)
        summed = acc_s[h] * shrink + jnp.dot(
            weights.astype(jnp.bfloat16), block_values, preferred_element_type=jnp.float32
        )
        m_s[h] = jnp.broadcast_to(highest, (rows, width))
        l_s[h] = jnp.broadcast_to(total, (rows, width))
        acc_s[h] = summed

    def each_head(action):
        lax.fori_loop(0, heads, lambda h, c: (action(h), c)[1], 0)

    each_head(lambda h: attend(pos, h))

    def passing(hop, right_next, left_next):
        from_left = (pos + n - hop) % n
        from_right = (pos + hop) % n

        def forward(h):
            rightward(from_left, h, hop - 1, *full).wait_recv()
            rightward(from_left, h, hop, *right_next).start()
            leftward(from_right, h, hop - 1, *full).wait_recv()
            leftward(from_right, h, hop, *left_next).start()

        def work(h):
            attend(from_left, h)
            attend(from_right, h)

        each_head(forward)
        each_head(work)

    lax.fori_loop(1, half - 1, lambda hop, c: (passing(hop, full, full), c)[1], 0)
    passing(half - 1, key_part, value_part)

    opposite = (pos + half) % n
    for h in range(heads):
        rightward(opposite, h, half - 1, *key_part).wait_recv()
        leftward(opposite, h, half - 1, *value_part).wait_recv()
        attend(opposite, h)
        att[h, mine] = (acc_s[h] / jnp.maximum(l_s[h], 1.0)).astype(jnp.bfloat16)
        for offset in range(1, groups):
            att_copy(offset, h).start()

    own_load.wait()
    for offset in range(1, groups):
        weights_copy(offset).wait_recv()
    result = None
    for h in range(heads):
        for offset in range(1, groups):
            att_copy(offset, h).wait_recv()
        joined = jnp.concatenate([att[h, g] for g in range(groups)], axis=1)
        part = jnp.dot(
            joined, wall[h].reshape(groups * width, cols), preferred_element_type=jnp.float32
        )
        result = part if result is None else result + part
    out_ref[...] = result.astype(out_ref.dtype)

    for offset in range(1, groups):
        weights_copy(offset).wait_send()
        for h in range(heads):
            att_copy(offset, h).wait_send()

    def drain(hop):
        def one(h):
            rightward(pos, h, hop, *full).wait_send()
            leftward(pos, h, hop, *full).wait_send()

        each_head(one)

    lax.fori_loop(0, half - 1, lambda hop, c: (drain(hop), c)[1], 0)
    for h in range(heads):
        rightward(pos, h, half - 1, *key_part).wait_send()
        leftward(pos, h, half - 1, *value_part).wait_send()


def body(
    tokens, qkv_weight, q_gain, k_gain, out_weight,
    query_cluster, key_cluster, query_slot, key_slot, pairs,
):
    n = lax.axis_size("seq")
    groups = lax.axis_size("head")
    rows, depth = tokens.shape
    heads = pairs.shape[0]
    width = q_gain.shape[0]
    key_clusters = key_slot.shape[1]
    members = query_slot.shape[1]
    slots = -(-key_clusters // LANES) * LANES
    cols = out_weight.shape[1] // groups

    ids = jnp.arange(slots, dtype=jnp.int32)
    listed = jnp.any(pairs[:, :, :, None] == ids, axis=2)
    member_ids = jnp.arange(members, dtype=jnp.int32)
    placed = query_slot[:, :, None] == member_ids
    named = query_cluster == member_ids
    owner = jnp.einsum(
        "htc,hcr->htr", named.astype(jnp.bfloat16), placed.astype(jnp.bfloat16),
        preferred_element_type=jnp.float32,
    ).astype(jnp.bfloat16)
    allowed = jnp.einsum(
        "htr,hrs->hts", owner, listed.astype(jnp.bfloat16), preferred_element_type=jnp.float32
    )
    neg = jnp.where(allowed > 0.5, 0.0, NEG).astype(jnp.bfloat16)
    cluster_ids = jnp.arange(key_clusters, dtype=jnp.int32)
    located = jnp.sum(
        jnp.where(key_cluster == cluster_ids, key_slot[:, None, :], 0), axis=2
    ).astype(jnp.bfloat16)
    info = located.reshape(heads, rows // LANES, LANES)
    info = jnp.pad(info, ((0, 0), (0, INFO - rows // LANES), (0, 0)))

    vmem = pl.BlockSpec(memory_space=pltpu.VMEM)
    anywhere = pl.BlockSpec(memory_space=pl.ANY)
    dma = pltpu.SemaphoreType.DMA
    bf16 = jnp.bfloat16
    return pl.pallas_call(
        functools.partial(kernel, n, groups),
        out_shape=jax.ShapeDtypeStruct((rows, cols), bf16),
        in_specs=[anywhere, anywhere, vmem, vmem, anywhere, vmem, vmem],
        out_specs=vmem,
        scratch_shapes=[
            pltpu.VMEM((rows, depth), bf16),
            pltpu.VMEM((3, depth, heads * width), bf16),
            pltpu.VMEM((n, heads, 2 * rows + INFO, width), bf16),
            pltpu.VMEM((heads, rows, width), bf16),
            pltpu.VMEM((heads, rows, width), jnp.float32),
            pltpu.VMEM((heads, rows, width), jnp.float32),
            pltpu.VMEM((heads, rows, width), jnp.float32),
            pltpu.VMEM((heads, groups, rows, width), bf16),
            pltpu.VMEM((heads, groups, width, cols), bf16),
            dma((5,)),
            dma((n // 2, heads)),
            dma((n // 2, heads)),
            dma((n // 2, heads)),
            dma((n // 2, heads)),
            dma((groups, heads)),
            dma((groups, heads)),
            dma((groups,)),
            dma((groups,)),
        ],
        compiler_params=pltpu.CompilerParams(
            collective_id=0, has_side_effects=True, vmem_limit_bytes=56 * 1024 * 1024
        ),
        cost_estimate=pl.CostEstimate(
            flops=2 * rows * depth * 4 * heads * width, bytes_accessed=12 * 1024 * 1024,
            transcendentals=heads * rows * rows * n,
        ),
    )(
        tokens,
        qkv_weight.transpose(1, 0, 2),
        q_gain.reshape(1, width),
        k_gain.reshape(1, width),
        out_weight.reshape(heads, width, out_weight.shape[1]),
        neg,
        info,
    )


def solution(mesh):
    placed = (
        P("seq", None),
        P(None, None, "head"),
        P(),
        P(),
        P("head", None),
        P("head", "seq", None),
        P("head", "seq", None),
        P("head", None),
        P("head", None),
        P("head", None, None),
    )
    return jax.shard_map(
        body, mesh=mesh, in_specs=placed, out_specs=P("seq", "head"), check_vma=False
    )
```

```python
import functools
import math

import jax
import jax.numpy as jnp
from jax import lax
from jax.experimental import pallas as pl
from jax.experimental.pallas import tpu as pltpu
from jax.sharding import PartitionSpec as P

EPSILON = 1e-06
NEG = -2e30
START = -1e30
MESH = pl.DeviceIdType.MESH
LANES = 128
INFO = 16


def normalize(projected, gain):
    mean_square = jnp.mean(projected * projected, axis=-1, keepdims=True)
    return projected * lax.rsqrt(mean_square + EPSILON) * gain


def ring_index(position, n):
    return jnp.where(position < n // 2, 2 * position, 2 * (n - 1 - position) + 1)


def look_up(labels, table_ref, h):
    found = jnp.zeros(labels.shape, jnp.int32)
    for c in range(table_ref.shape[1]):
        found = jnp.where(labels == c, table_ref[h, c], found)
    return found


def kernel(
    n, groups, tok_ref, wqkv_ref, qg_ref, kg_ref, wout_ref, qc_ref, kc_ref, qslot_ref, kslot_ref,
    pairs_ref, out_ref, tok_v, w_v, kv, q_v, neg_s, m_s, l_s, acc_s, att, wall,
    load_sem, right_send, right_recv, left_send, left_recv,
    att_send, att_recv, wt_send, wt_recv,
):
    heads, rows, width = q_v.shape
    cols = out_ref.shape[1]
    half = n // 2
    seq = lax.axis_index("seq")
    mine = lax.axis_index("head")
    pos = jnp.where(seq % 2 == 0, seq // 2, n - 1 - seq // 2)
    right = ring_index((pos + 1) % n, n)
    left = ring_index((pos + n - 1) % n, n)

    tok_load = pltpu.make_async_copy(tok_ref, tok_v, load_sem.at[0])
    tok_load.start()
    w_loads = [pltpu.make_async_copy(wqkv_ref.at[j], w_v.at[j], load_sem.at[1 + j]) for j in range(3)]
    for j in (1, 2, 0):
        w_loads[j].start()
    own_cols = pl.ds(pl.multiple_of(mine * cols, LANES), cols)
    own_load = pltpu.make_async_copy(wout_ref.at[:, :, own_cols], wall.at[:, mine], load_sem.at[4])
    own_load.start()

    barrier = pltpu.get_barrier_semaphore()
    for neighbour in (left, right):
        pl.semaphore_signal(barrier, inc=1, device_id={"seq": neighbour}, device_id_type=MESH)
    for offset in range(1, groups):
        pl.semaphore_signal(
            barrier, inc=1, device_id={"head": (mine + offset) % groups}, device_id_type=MESH
        )

    def rightward(slot, h, hop, low, size):
        part = kv.at[slot, h, pl.ds(low, size)]
        return pltpu.make_async_remote_copy(
            src_ref=part, dst_ref=part, send_sem=right_send.at[hop, h],
            recv_sem=right_recv.at[hop, h], device_id={"seq": right}, device_id_type=MESH,
        )

    def leftward(slot, h, hop, low, size):
        part = kv.at[slot, h, pl.ds(low, size)]
        return pltpu.make_async_remote_copy(
            src_ref=part, dst_ref=part, send_sem=left_send.at[hop, h],
            recv_sem=left_recv.at[hop, h], device_id={"seq": left}, device_id_type=MESH,
        )

    full = (0, 2 * rows + INFO)
    key_part = (rows, rows + INFO)
    value_part = (0, rows)

    def weights_copy(offset):
        peer = (mine + offset) % groups
        peer_cols = pl.ds(pl.multiple_of(peer * cols, LANES), cols)
        return pltpu.make_async_remote_copy(
            src_ref=wout_ref.at[:, :, peer_cols], dst_ref=wall.at[:, mine],
            send_sem=wt_send.at[offset], recv_sem=wt_recv.at[offset],
            device_id={"head": peer}, device_id_type=MESH,
        )

    near = mine + 1 - 2 * (mine % 2)
    far = (mine + 2) % groups

    def att_copy(kind, h):
        block = far if kind == 2 else mine
        return pltpu.make_async_remote_copy(
            src_ref=att.at[h, block], dst_ref=att.at[h, block],
            send_sem=att_send.at[kind, h], recv_sem=att_recv.at[kind, h],
            device_id={"head": far if kind == 1 else near}, device_id_type=MESH,
        )

    for h in range(heads):
        placed = look_up(kc_ref[h], kslot_ref, h).astype(jnp.float32)
        lines = [placed[:, r * LANES : (r + 1) * LANES] for r in range(rows // LANES)]
        lines.append(jnp.zeros((INFO - rows // LANES, LANES), jnp.float32))
        kv[pos, h, pl.ds(2 * rows, INFO)] = jnp.concatenate(lines, axis=0).astype(jnp.bfloat16)

    tok_load.wait()
    w_loads[1].wait()
    keys = jnp.dot(tok_v[...], w_v[1], preferred_element_type=jnp.float32)
    for h in range(heads):
        kv[pos, h, pl.ds(rows, rows)] = normalize(
            keys[:, h * width : (h + 1) * width], kg_ref[...]
        ).astype(jnp.bfloat16)
    w_loads[2].wait()
    values = jnp.dot(tok_v[...], w_v[2], preferred_element_type=jnp.float32)
    for h in range(heads):
        kv[pos, h, pl.ds(0, rows)] = values[:, h * width : (h + 1) * width].astype(jnp.bfloat16)

    pl.semaphore_wait(barrier, 1 + groups)
    for h in range(heads):
        rightward(pos, h, 0, *full).start()
        leftward(pos, h, 0, *full).start()
    for offset in range(1, groups):
        weights_copy(offset).start()

    w_loads[0].wait()
    queries = jnp.dot(tok_v[...], w_v[0], preferred_element_type=jnp.float32)
    for h in range(heads):
        q_v[h] = normalize(queries[:, h * width : (h + 1) * width], qg_ref[...]).astype(
            jnp.bfloat16
        )
    members, lists = pairs_ref.shape[1:]
    slots = neg_s.shape[2]
    padded = -(-members // LANES) * LANES
    member_ids = lax.broadcasted_iota(jnp.int32, (padded, rows), 0)
    slot_ids = lax.broadcasted_iota(jnp.int32, (members, slots), 1)
    for h in range(heads):
        owners = look_up(qc_ref[h], qslot_ref, h)
        owned = jnp.where(member_ids == owners, 1.0, 0.0).T.astype(jnp.bfloat16)
        entries = pairs_ref[h]
        listed = jnp.zeros((members, slots), jnp.float32)
        for k in range(lists):
            listed = jnp.where(entries[:, k : k + 1] == slot_ids, 1.0, listed)
        if padded > members:
            blank = jnp.zeros((padded - members, slots), jnp.float32)
            listed = jnp.concatenate([listed, blank], axis=0)
        allowed = jnp.dot(owned, listed.astype(jnp.bfloat16), preferred_element_type=jnp.float32)
        neg_s[h] = jnp.where(allowed > 0.5, 0.0, NEG).astype(jnp.bfloat16)
    m_s[...] = jnp.full(m_s.shape, START, jnp.float32)
    l_s[...] = jnp.zeros(l_s.shape, jnp.float32)
    acc_s[...] = jnp.zeros(acc_s.shape, jnp.float32)
    factor = math.log2(math.e) / math.sqrt(width)

    def attend(slot, h):
        block_values = kv[slot, h, pl.ds(0, rows)]
        block_keys = kv[slot, h, pl.ds(rows, rows)]
        info = kv[slot, h, pl.ds(2 * rows, INFO)].astype(jnp.float32)
        row = jnp.concatenate([info[r : r + 1, :] for r in range(rows // LANES)], axis=1)
        ids = lax.broadcasted_iota(jnp.int32, (slots, rows), 0).astype(jnp.float32)
        owner = jnp.where(ids == row, 1.0, 0.0).astype(jnp.bfloat16)
        scores = lax.dot_general(
            q_v[h], block_keys, (((1,), (1,)), ((), ())), preferred_element_type=jnp.float32
        ) + jnp.dot(neg_s[h], owner, preferred_element_type=jnp.float32)
        before = m_s[h][:, :1]
        highest = jnp.maximum(before, jnp.max(scores, axis=1, keepdims=True))
        weights = jnp.exp2((scores - highest) * factor)
        shrink = jnp.exp2((before - highest) * factor)
        total = l_s[h][:, :1] * shrink + jnp.sum(weights, axis=1, keepdims=True)
        summed = acc_s[h] * shrink + jnp.dot(
            weights.astype(jnp.bfloat16), block_values, preferred_element_type=jnp.float32
        )
        m_s[h] = jnp.broadcast_to(highest, (rows, width))
        l_s[h] = jnp.broadcast_to(total, (rows, width))
        acc_s[h] = summed

    def each_head(action):
        lax.fori_loop(0, heads, lambda h, c: (action(h), c)[1], 0)

    each_head(lambda h: attend(pos, h))

    def passing(hop, right_next, left_next):
        from_left = (pos + n - hop) % n
        from_right = (pos + hop) % n

        def forward(h):
            rightward(from_left, h, hop - 1, *full).wait_recv()
            rightward(from_left, h, hop, *right_next).start()
            leftward(from_right, h, hop - 1, *full).wait_recv()
            leftward(from_right, h, hop, *left_next).start()

        def work(h):
            attend(from_left, h)
            attend(from_right, h)

        each_head(forward)
        each_head(work)

    lax.fori_loop(1, half - 1, lambda hop, c: (passing(hop, full, full), c)[1], 0)
    passing(half - 1, key_part, value_part)

    opposite = (pos + half) % n
    for h in range(heads):
        rightward(opposite, h, half - 1, *key_part).wait_recv()
        leftward(opposite, h, half - 1, *value_part).wait_recv()
        attend(opposite, h)
        att[h, mine] = (acc_s[h] / jnp.maximum(l_s[h], 1.0)).astype(jnp.bfloat16)
        att_copy(0, h).start()
        att_copy(1, h).start()
        if h > 0:
            att_copy(1, h - 1).wait_recv()
            att_copy(2, h - 1).start()

    own_load.wait()
    for offset in range(1, groups):
        weights_copy(offset).wait_recv()
    result = None
    for h in range(heads):
        if h == heads - 1:
            att_copy(1, h).wait_recv()
            att_copy(2, h).start()
        att_copy(0, h).wait_recv()
        att_copy(2, h).wait_recv()
        joined = jnp.concatenate([att[h, g] for g in range(groups)], axis=1)
        part = jnp.dot(
            joined, wall[h].reshape(groups * width, cols), preferred_element_type=jnp.float32
        )
        result = part if result is None else result + part
    out_ref[...] = result.astype(out_ref.dtype)

    for offset in range(1, groups):
        weights_copy(offset).wait_send()
    for h in range(heads):
        for kind in range(3):
            att_copy(kind, h).wait_send()

    def drain(hop):
        def one(h):
            rightward(pos, h, hop, *full).wait_send()
            leftward(pos, h, hop, *full).wait_send()

        each_head(one)

    lax.fori_loop(0, half - 1, lambda hop, c: (drain(hop), c)[1], 0)
    for h in range(heads):
        rightward(pos, h, half - 1, *key_part).wait_send()
        leftward(pos, h, half - 1, *value_part).wait_send()


def body(
    tokens, qkv_weight, q_gain, k_gain, out_weight,
    query_cluster, key_cluster, query_slot, key_slot, pairs,
):
    n = lax.axis_size("seq")
    groups = lax.axis_size("head")
    rows, depth = tokens.shape
    heads = pairs.shape[0]
    width = q_gain.shape[0]
    key_clusters = key_slot.shape[1]
    slots = -(-key_clusters // LANES) * LANES
    cols = out_weight.shape[1] // groups

    vmem = pl.BlockSpec(memory_space=pltpu.VMEM)
    smem = pl.BlockSpec(memory_space=pltpu.SMEM)
    anywhere = pl.BlockSpec(memory_space=pl.ANY)
    dma = pltpu.SemaphoreType.DMA
    bf16 = jnp.bfloat16
    return pl.pallas_call(
        functools.partial(kernel, n, groups),
        out_shape=jax.ShapeDtypeStruct((rows, cols), bf16),
        in_specs=[anywhere, anywhere, vmem, vmem, anywhere, vmem, vmem, smem, smem, vmem],
        out_specs=vmem,
        scratch_shapes=[
            pltpu.VMEM((rows, depth), bf16),
            pltpu.VMEM((3, depth, heads * width), bf16),
            pltpu.VMEM((n, heads, 2 * rows + INFO, width), bf16),
            pltpu.VMEM((heads, rows, width), bf16),
            pltpu.VMEM((heads, rows, slots), bf16),
            pltpu.VMEM((heads, rows, width), jnp.float32),
            pltpu.VMEM((heads, rows, width), jnp.float32),
            pltpu.VMEM((heads, rows, width), jnp.float32),
            pltpu.VMEM((heads, groups, rows, width), bf16),
            pltpu.VMEM((heads, groups, width, cols), bf16),
            dma((5,)),
            dma((n // 2, heads)),
            dma((n // 2, heads)),
            dma((n // 2, heads)),
            dma((n // 2, heads)),
            dma((3, heads)),
            dma((3, heads)),
            dma((groups,)),
            dma((groups,)),
        ],
        compiler_params=pltpu.CompilerParams(
            collective_id=0, has_side_effects=True, vmem_limit_bytes=56 * 1024 * 1024
        ),
        cost_estimate=pl.CostEstimate(
            flops=2 * rows * depth * 4 * heads * width, bytes_accessed=12 * 1024 * 1024,
            transcendentals=heads * rows * rows * n,
        ),
    )(
        tokens,
        qkv_weight.transpose(1, 0, 2),
        q_gain.reshape(1, width),
        k_gain.reshape(1, width),
        out_weight.reshape(heads, width, out_weight.shape[1]),
        query_cluster.transpose(0, 2, 1),
        key_cluster.transpose(0, 2, 1),
        query_slot,
        key_slot,
        pairs,
    )


def solution(mesh):
    placed = (
        P("seq", None),
        P(None, None, "head"),
        P(),
        P(),
        P("head", None),
        P("head", "seq", None),
        P("head", "seq", None),
        P("head", None),
        P("head", None),
        P("head", None, None),
    )
    return jax.shard_map(
        body, mesh=mesh, in_specs=placed, out_specs=P("seq", "head"), check_vma=False
    )
```

```python
import functools
import math

import jax
import jax.numpy as jnp
from jax import lax
from jax.experimental import pallas as pl
from jax.experimental.pallas import tpu as pltpu
from jax.sharding import PartitionSpec as P

EPSILON = 1e-06
NEG = -2e30
START = -1e30
MESH = pl.DeviceIdType.MESH
LANES = 128
INFO = 16


def normalize(projected, gain):
    mean_square = jnp.mean(projected * projected, axis=-1, keepdims=True)
    return projected * lax.rsqrt(mean_square + EPSILON) * gain


def ring_index(position, n):
    return jnp.where(position < n // 2, 2 * position, 2 * (n - 1 - position) + 1)


def look_up(labels, table_ref, h):
    found = jnp.zeros(labels.shape, jnp.int32)
    for c in range(table_ref.shape[1]):
        found = jnp.where(labels == c, table_ref[h, c], found)
    return found


def kernel(
    n, groups, tok_ref, wqkv_ref, qg_ref, kg_ref, wout_ref, qc_ref, kc_ref, qslot_ref, kslot_ref,
    pairs_ref, out_ref, tok_v, w_v, kv, q_v, neg_s, m_s, l_s, acc_s, att, wall,
    load_sem, right_send, right_recv, left_send, left_recv,
    att_send, att_recv, wt_send, wt_recv,
):
    heads, rows, width = q_v.shape
    cols = out_ref.shape[1]
    half = n // 2
    seq = lax.axis_index("seq")
    mine = lax.axis_index("head")
    pos = jnp.where(seq % 2 == 0, seq // 2, n - 1 - seq // 2)
    right = ring_index((pos + 1) % n, n)
    left = ring_index((pos + n - 1) % n, n)

    tok_load = pltpu.make_async_copy(tok_ref, tok_v, load_sem.at[0])
    tok_load.start()
    w_loads = [pltpu.make_async_copy(wqkv_ref.at[j], w_v.at[j], load_sem.at[1 + j]) for j in range(3)]
    w_loads[1].start()
    own_cols = pl.ds(pl.multiple_of(mine * cols, LANES), cols)
    own_load = pltpu.make_async_copy(wout_ref.at[:, :, own_cols], wall.at[:, mine], load_sem.at[4])
    barrier = pltpu.get_barrier_semaphore()
    for neighbour in (left, right):
        pl.semaphore_signal(barrier, inc=1, device_id={"seq": neighbour}, device_id_type=MESH)
    for offset in range(1, groups):
        pl.semaphore_signal(
            barrier, inc=1, device_id={"head": (mine + offset) % groups}, device_id_type=MESH
        )

    def rightward(slot, h, hop, low, size):
        part = kv.at[slot, h, pl.ds(low, size)]
        return pltpu.make_async_remote_copy(
            src_ref=part, dst_ref=part, send_sem=right_send.at[hop, h],
            recv_sem=right_recv.at[hop, h], device_id={"seq": right}, device_id_type=MESH,
        )

    def leftward(slot, h, hop, low, size):
        part = kv.at[slot, h, pl.ds(low, size)]
        return pltpu.make_async_remote_copy(
            src_ref=part, dst_ref=part, send_sem=left_send.at[hop, h],
            recv_sem=left_recv.at[hop, h], device_id={"seq": left}, device_id_type=MESH,
        )

    full = (0, 2 * rows + INFO)
    key_part = (rows, rows + INFO)
    value_part = (0, rows)

    def weights_copy(offset):
        peer = (mine + offset) % groups
        peer_cols = pl.ds(pl.multiple_of(peer * cols, LANES), cols)
        return pltpu.make_async_remote_copy(
            src_ref=wout_ref.at[:, :, peer_cols], dst_ref=wall.at[:, mine],
            send_sem=wt_send.at[offset], recv_sem=wt_recv.at[offset],
            device_id={"head": peer}, device_id_type=MESH,
        )

    near = mine + 1 - 2 * (mine % 2)
    far = (mine + 2) % groups

    def att_copy(kind, h):
        block = far if kind == 2 else mine
        return pltpu.make_async_remote_copy(
            src_ref=att.at[h, block], dst_ref=att.at[h, block],
            send_sem=att_send.at[kind, h], recv_sem=att_recv.at[kind, h],
            device_id={"head": far if kind == 1 else near}, device_id_type=MESH,
        )

    for h in range(heads):
        placed = look_up(kc_ref[h], kslot_ref, h).astype(jnp.float32)
        lines = [placed[:, r * LANES : (r + 1) * LANES] for r in range(rows // LANES)]
        lines.append(jnp.zeros((INFO - rows // LANES, LANES), jnp.float32))
        kv[pos, h, pl.ds(2 * rows, INFO)] = jnp.concatenate(lines, axis=0).astype(jnp.bfloat16)

    tok_load.wait()
    w_loads[1].wait()
    w_loads[2].start()
    w_loads[0].start()
    keys = jnp.dot(tok_v[...], w_v[1], preferred_element_type=jnp.float32)
    for h in range(heads):
        kv[pos, h, pl.ds(rows, rows)] = normalize(
            keys[:, h * width : (h + 1) * width], kg_ref[...]
        ).astype(jnp.bfloat16)
    pl.semaphore_wait(barrier, 1 + groups)
    for h in range(heads):
        rightward(pos, h, 0, *key_part).start()
        leftward(pos, h, 0, *key_part).start()
    w_loads[2].wait()
    values = jnp.dot(tok_v[...], w_v[2], preferred_element_type=jnp.float32)
    for h in range(heads):
        kv[pos, h, pl.ds(0, rows)] = values[:, h * width : (h + 1) * width].astype(jnp.bfloat16)

    for h in range(heads):
        rightward(pos, h, 0, *value_part).start()
        leftward(pos, h, 0, *value_part).start()
    own_load.start()
    for offset in range(1, groups):
        weights_copy(offset).start()

    w_loads[0].wait()
    queries = jnp.dot(tok_v[...], w_v[0], preferred_element_type=jnp.float32)
    for h in range(heads):
        q_v[h] = normalize(queries[:, h * width : (h + 1) * width], qg_ref[...]).astype(
            jnp.bfloat16
        )
    members, lists = pairs_ref.shape[1:]
    slots = neg_s.shape[2]
    padded = -(-members // LANES) * LANES
    member_ids = lax.broadcasted_iota(jnp.int32, (padded, rows), 0)
    slot_ids = lax.broadcasted_iota(jnp.int32, (members, slots), 1)
    for h in range(heads):
        owners = look_up(qc_ref[h], qslot_ref, h)
        owned = jnp.where(member_ids == owners, 1.0, 0.0).T.astype(jnp.bfloat16)
        entries = pairs_ref[h]
        listed = jnp.zeros((members, slots), jnp.float32)
        for k in range(lists):
            listed = jnp.where(entries[:, k : k + 1] == slot_ids, 1.0, listed)
        if padded > members:
            blank = jnp.zeros((padded - members, slots), jnp.float32)
            listed = jnp.concatenate([listed, blank], axis=0)
        allowed = jnp.dot(owned, listed.astype(jnp.bfloat16), preferred_element_type=jnp.float32)
        neg_s[h] = jnp.where(allowed > 0.5, 0.0, NEG).astype(jnp.bfloat16)
    m_s[...] = jnp.full(m_s.shape, START, jnp.float32)
    l_s[...] = jnp.zeros(l_s.shape, jnp.float32)
    acc_s[...] = jnp.zeros(acc_s.shape, jnp.float32)
    factor = math.log2(math.e) / math.sqrt(width)

    def attend(slot, h):
        block_values = kv[slot, h, pl.ds(0, rows)]
        block_keys = kv[slot, h, pl.ds(rows, rows)]
        info = kv[slot, h, pl.ds(2 * rows, INFO)].astype(jnp.float32)
        row = jnp.concatenate([info[r : r + 1, :] for r in range(rows // LANES)], axis=1)
        ids = lax.broadcasted_iota(jnp.int32, (slots, rows), 0).astype(jnp.float32)
        owner = jnp.where(ids == row, 1.0, 0.0).astype(jnp.bfloat16)
        scores = lax.dot_general(
            q_v[h], block_keys, (((1,), (1,)), ((), ())), preferred_element_type=jnp.float32
        ) + jnp.dot(neg_s[h], owner, preferred_element_type=jnp.float32)
        before = m_s[h][:, :1]
        highest = jnp.maximum(before, jnp.max(scores, axis=1, keepdims=True))
        weights = jnp.exp2((scores - highest) * factor)
        shrink = jnp.exp2((before - highest) * factor)
        total = l_s[h][:, :1] * shrink + jnp.sum(weights, axis=1, keepdims=True)
        summed = acc_s[h] * shrink + jnp.dot(
            weights.astype(jnp.bfloat16), block_values, preferred_element_type=jnp.float32
        )
        m_s[h] = jnp.broadcast_to(highest, (rows, width))
        l_s[h] = jnp.broadcast_to(total, (rows, width))
        acc_s[h] = summed

    def each_head(action):
        lax.fori_loop(0, heads, lambda h, c: (action(h), c)[1], 0)

    each_head(lambda h: attend(pos, h))

    def passing(hop, right_next, left_next):
        from_left = (pos + n - hop) % n
        from_right = (pos + hop) % n

        def forward(h):
            rightward(from_left, h, hop - 1, *full).wait_recv()
            rightward(from_left, h, hop, *right_next).start()
            leftward(from_right, h, hop - 1, *full).wait_recv()
            leftward(from_right, h, hop, *left_next).start()
            attend(from_left, h)
            attend(from_right, h)

        each_head(forward)

    lax.fori_loop(1, half - 1, lambda hop, c: (passing(hop, full, full), c)[1], 0)
    passing(half - 1, key_part, value_part)

    opposite = (pos + half) % n
    for h in range(heads):
        rightward(opposite, h, half - 1, *key_part).wait_recv()
        leftward(opposite, h, half - 1, *value_part).wait_recv()
        attend(opposite, h)
        att[h, mine] = (acc_s[h] / jnp.maximum(l_s[h], 1.0)).astype(jnp.bfloat16)
        att_copy(0, h).start()
        att_copy(1, h).start()
        if h > 0:
            att_copy(1, h - 1).wait_recv()
            att_copy(2, h - 1).start()

    own_load.wait()
    for offset in range(1, groups):
        weights_copy(offset).wait_recv()
    result = None
    for h in range(heads):
        if h == heads - 1:
            att_copy(1, h).wait_recv()
            att_copy(2, h).start()
        att_copy(0, h).wait_recv()
        att_copy(2, h).wait_recv()
        joined = jnp.concatenate([att[h, g] for g in range(groups)], axis=1)
        part = jnp.dot(
            joined, wall[h].reshape(groups * width, cols), preferred_element_type=jnp.float32
        )
        result = part if result is None else result + part
    out_ref[...] = result.astype(out_ref.dtype)

    for offset in range(1, groups):
        weights_copy(offset).wait_send()
    for h in range(heads):
        for kind in range(3):
            att_copy(kind, h).wait_send()

    def drain(hop):
        def one(h):
            rightward(pos, h, hop, *full).wait_send()
            leftward(pos, h, hop, *full).wait_send()

        each_head(one)

    lax.fori_loop(0, half - 1, lambda hop, c: (drain(hop), c)[1], 0)
    for h in range(heads):
        rightward(pos, h, half - 1, *key_part).wait_send()
        leftward(pos, h, half - 1, *value_part).wait_send()


def body(
    tokens, qkv_weight, q_gain, k_gain, out_weight,
    query_cluster, key_cluster, query_slot, key_slot, pairs,
):
    n = lax.axis_size("seq")
    groups = lax.axis_size("head")
    rows, depth = tokens.shape
    heads = pairs.shape[0]
    width = q_gain.shape[0]
    key_clusters = key_slot.shape[1]
    slots = -(-key_clusters // LANES) * LANES
    cols = out_weight.shape[1] // groups

    vmem = pl.BlockSpec(memory_space=pltpu.VMEM)
    smem = pl.BlockSpec(memory_space=pltpu.SMEM)
    anywhere = pl.BlockSpec(memory_space=pl.ANY)
    dma = pltpu.SemaphoreType.DMA
    bf16 = jnp.bfloat16
    return pl.pallas_call(
        functools.partial(kernel, n, groups),
        out_shape=jax.ShapeDtypeStruct((rows, cols), bf16),
        in_specs=[anywhere, anywhere, vmem, vmem, anywhere, vmem, vmem, smem, smem, vmem],
        out_specs=vmem,
        scratch_shapes=[
            pltpu.VMEM((rows, depth), bf16),
            pltpu.VMEM((3, depth, heads * width), bf16),
            pltpu.VMEM((n, heads, 2 * rows + INFO, width), bf16),
            pltpu.VMEM((heads, rows, width), bf16),
            pltpu.VMEM((heads, rows, slots), bf16),
            pltpu.VMEM((heads, rows, width), jnp.float32),
            pltpu.VMEM((heads, rows, width), jnp.float32),
            pltpu.VMEM((heads, rows, width), jnp.float32),
            pltpu.VMEM((heads, groups, rows, width), bf16),
            pltpu.VMEM((heads, groups, width, cols), bf16),
            dma((5,)),
            dma((n // 2, heads)),
            dma((n // 2, heads)),
            dma((n // 2, heads)),
            dma((n // 2, heads)),
            dma((3, heads)),
            dma((3, heads)),
            dma((groups,)),
            dma((groups,)),
        ],
        compiler_params=pltpu.CompilerParams(
            collective_id=0, has_side_effects=True, vmem_limit_bytes=56 * 1024 * 1024
        ),
        cost_estimate=pl.CostEstimate(
            flops=2 * rows * depth * 4 * heads * width, bytes_accessed=12 * 1024 * 1024,
            transcendentals=heads * rows * rows * n,
        ),
    )(
        tokens,
        qkv_weight.transpose(1, 0, 2),
        q_gain.reshape(1, width),
        k_gain.reshape(1, width),
        out_weight.reshape(heads, width, out_weight.shape[1]),
        query_cluster.transpose(0, 2, 1),
        key_cluster.transpose(0, 2, 1),
        query_slot,
        key_slot,
        pairs,
    )


def solution(mesh):
    placed = (
        P("seq", None),
        P(None, None, "head"),
        P(),
        P(),
        P("head", None),
        P("head", "seq", None),
        P("head", "seq", None),
        P("head", None),
        P("head", None),
        P("head", None, None),
    )
    return jax.shard_map(
        body, mesh=mesh, in_specs=placed, out_specs=P("seq", "head"), check_vma=False
    )
```

```python
import functools
import math

import jax
import jax.numpy as jnp
from jax import lax
from jax.experimental import pallas as pl
from jax.experimental.pallas import tpu as pltpu
from jax.sharding import PartitionSpec as P

EPSILON = 1e-06
NEG = -2e30
START = -1e30
MESH = pl.DeviceIdType.MESH
LANES = 128
INFO = 16


def normalize(projected, gain):
    mean_square = jnp.mean(projected * projected, axis=-1, keepdims=True)
    return projected * lax.rsqrt(mean_square + EPSILON) * gain


def look_up(labels, table_ref, h):
    found = jnp.zeros(labels.shape, jnp.int32)
    for c in range(table_ref.shape[1]):
        found = jnp.where(labels == c, table_ref[h, c], found)
    return found


def kernel(
    n, groups, tok_ref, wqkv_ref, qg_ref, kg_ref, wout_ref, qc_ref, kc_ref, qslot_ref, kslot_ref,
    pairs_ref, out_ref, tok_v, w_v, kv, q_v, neg_s, m_s, l_s, acc_s, att, wall,
    load_sem, left_send, right_send, side_send, core_send, col_recv, side_recv, core_recv,
    swap_send, swap_recv, att_send, att_recv, wt_send, wt_recv,
):
    heads, rows, width = acc_s.shape
    cols = out_ref.shape[1]
    layers = n // 2
    seq = lax.axis_index("seq")
    mine = lax.axis_index("head")
    layer, side = seq // 2, seq % 2
    active = mine % 2 == layer % 2
    near = mine + 1 - 2 * (mine % 2)
    far = (mine + 2) % groups
    other_layer = layer + 1 - 2 * (layer % 2)
    swap_seq = other_layer * 2 + side
    turn = jnp.where(active, 0, 1)

    tok_load = pltpu.make_async_copy(tok_ref, tok_v, load_sem.at[0])
    tok_load.start()
    w_loads = [pltpu.make_async_copy(wqkv_ref.at[j], w_v.at[j], load_sem.at[1 + j]) for j in range(3)]
    w_loads[1].start()
    own_cols = pl.ds(pl.multiple_of(mine * cols, LANES), cols)
    own_load = pltpu.make_async_copy(wout_ref.at[:, :, own_cols], wall.at[:, mine], load_sem.at[4])
    barrier = pltpu.get_barrier_semaphore()
    met = 1 + groups
    for step in (-2, -1, 1, 2):
        reached = (layer + step >= 0) & (layer + step < layers)
        met = met + jnp.where(reached, 1, 0)

        @pl.when(reached)
        def _():
            pl.semaphore_signal(
                barrier, inc=1, device_id={"seq": seq + 2 * step}, device_id_type=MESH
            )

    pl.semaphore_signal(
        barrier, inc=1, device_id={"seq": layer * 2 + 1 - side}, device_id_type=MESH
    )
    pl.semaphore_signal(
        barrier, inc=1, device_id={"seq": swap_seq, "head": near}, device_id_type=MESH
    )
    for offset in range(1, groups):
        pl.semaphore_signal(
            barrier, inc=1, device_id={"head": (mine + offset) % groups}, device_id_type=MESH
        )

    def send(source, slot, h, part, send_sem, recv_sem, device):
        low, size = part
        return pltpu.make_async_remote_copy(
            src_ref=kv.at[source, h, pl.ds(low, size)], dst_ref=kv.at[slot, h, pl.ds(low, size)],
            send_sem=send_sem, recv_sem=recv_sem, device_id=device, device_id_type=MESH,
        )

    def column(source, j, h, part, step):
        sems = left_send if step < 0 else right_send
        return send(
            source, j * 2 + side, h, part, sems.at[j, h], col_recv.at[j, h],
            {"seq": seq + 2 * step},
        )

    def across(source, j, h, part):
        return send(
            source, j * 2 + side, h, part, side_send.at[j, h], side_recv.at[j, h],
            {"seq": layer * 2 + 1 - side},
        )

    def to_core(source, slot, h, part):
        return send(
            source, slot, h, part, core_send.at[slot, h], core_recv.at[slot, h], {"head": near}
        )

    def swap_copy(kind, h):
        source, target = (
            (q_v.at[0, h], q_v.at[1, h]),
            (neg_s.at[0, h], neg_s.at[1, h]),
            (q_v.at[0, h], att.at[h, near]),
        )[kind]
        return pltpu.make_async_remote_copy(
            src_ref=source, dst_ref=target,
            send_sem=swap_send.at[kind, h], recv_sem=swap_recv.at[kind, h],
            device_id={"seq": swap_seq, "head": near}, device_id_type=MESH,
        )

    full = (0, 2 * rows + INFO)
    key_part = (rows, rows + INFO)
    value_part = (0, rows)

    def weights_copy(offset):
        peer = (mine + offset) % groups
        peer_cols = pl.ds(pl.multiple_of(peer * cols, LANES), cols)
        return pltpu.make_async_remote_copy(
            src_ref=wout_ref.at[:, :, peer_cols], dst_ref=wall.at[:, mine],
            send_sem=wt_send.at[offset], recv_sem=wt_recv.at[offset],
            device_id={"head": peer}, device_id_type=MESH,
        )

    def att_copy(kind, h):
        block = far if kind == 2 else mine
        return pltpu.make_async_remote_copy(
            src_ref=att.at[h, block], dst_ref=att.at[h, block],
            send_sem=att_send.at[kind, h], recv_sem=att_recv.at[kind, h],
            device_id={"head": far if kind == 1 else near}, device_id_type=MESH,
        )

    for h in range(heads):
        placed = look_up(kc_ref[h], kslot_ref, h).astype(jnp.float32)
        lines = [placed[:, r * LANES : (r + 1) * LANES] for r in range(rows // LANES)]
        lines.append(jnp.zeros((INFO - rows // LANES, LANES), jnp.float32))
        kv[n, h, pl.ds(2 * rows, INFO)] = jnp.concatenate(lines, axis=0).astype(jnp.bfloat16)

    tok_load.wait()
    w_loads[1].wait()
    w_loads[2].start()
    w_loads[0].start()
    keys = jnp.dot(tok_v[...], w_v[1], preferred_element_type=jnp.float32)
    for h in range(heads):
        kv[n, h, pl.ds(rows, rows)] = normalize(
            keys[:, h * width : (h + 1) * width], kg_ref[...]
        ).astype(jnp.bfloat16)
    can_left = {step: layer - step >= 0 for step in (1, 2)}
    can_right = {step: layer + step < layers for step in (1, 2)}

    def each_own(part, action):
        for step in (1, 2):
            wanted = active if step == 2 else jnp.logical_not(active)
            for direction, allowed in ((-step, can_left[step]), (step, can_right[step])):

                @pl.when(wanted & allowed)
                def _():
                    for h in range(heads):
                        action(column(n, layer, h, part, direction))

        @pl.when(active)
        def _():
            for h in range(heads):
                action(across(n, layer, h, part))
                action(to_core(n, seq, h, part))

    pl.semaphore_wait(barrier, met)
    each_own(key_part, lambda copy: copy.start())
    w_loads[2].wait()
    values = jnp.dot(tok_v[...], w_v[2], preferred_element_type=jnp.float32)
    for h in range(heads):
        kv[n, h, pl.ds(0, rows)] = values[:, h * width : (h + 1) * width].astype(jnp.bfloat16)

    each_own(value_part, lambda copy: copy.start())
    own_load.start()
    for offset in range(1, groups):
        weights_copy(offset).start()

    w_loads[0].wait()
    queries = jnp.dot(tok_v[...], w_v[0], preferred_element_type=jnp.float32)
    for h in range(heads):
        q_v[0, h] = normalize(queries[:, h * width : (h + 1) * width], qg_ref[...]).astype(
            jnp.bfloat16
        )
    members, lists = pairs_ref.shape[1:]
    slots = neg_s.shape[3]
    padded = -(-members // LANES) * LANES
    member_ids = lax.broadcasted_iota(jnp.int32, (padded, rows), 0)
    slot_ids = lax.broadcasted_iota(jnp.int32, (members, slots), 1)
    for h in range(heads):
        owners = look_up(qc_ref[h], qslot_ref, h)
        owned = jnp.where(member_ids == owners, 1.0, 0.0).T.astype(jnp.bfloat16)
        entries = pairs_ref[h]
        listed = jnp.zeros((members, slots), jnp.float32)
        for k in range(lists):
            listed = jnp.where(entries[:, k : k + 1] == slot_ids, 1.0, listed)
        if padded > members:
            blank = jnp.zeros((padded - members, slots), jnp.float32)
            listed = jnp.concatenate([listed, blank], axis=0)
        allowed = jnp.dot(owned, listed.astype(jnp.bfloat16), preferred_element_type=jnp.float32)
        neg_s[0, h] = jnp.where(allowed > 0.5, 0.0, NEG).astype(jnp.bfloat16)

    @pl.when(jnp.logical_not(active))
    def _():
        for h in range(heads):
            swap_copy(0, h).start()
            swap_copy(1, h).start()

    m_s[...] = jnp.full(m_s.shape, START, jnp.float32)
    l_s[...] = jnp.zeros(l_s.shape, jnp.float32)
    acc_s[...] = jnp.zeros(acc_s.shape, jnp.float32)
    factor = math.log2(math.e) / math.sqrt(width)

    def attend(slot, h):
        block_values = kv[slot, h, pl.ds(0, rows)]
        block_keys = kv[slot, h, pl.ds(rows, rows)]
        info = kv[slot, h, pl.ds(2 * rows, INFO)].astype(jnp.float32)
        row = jnp.concatenate([info[r : r + 1, :] for r in range(rows // LANES)], axis=1)
        ids = lax.broadcasted_iota(jnp.int32, (slots, rows), 0).astype(jnp.float32)
        owner = jnp.where(ids == row, 1.0, 0.0).astype(jnp.bfloat16)
        scores = lax.dot_general(
            q_v[turn, h], block_keys, (((1,), (1,)), ((), ())), preferred_element_type=jnp.float32
        ) + jnp.dot(neg_s[turn, h], owner, preferred_element_type=jnp.float32)
        before = m_s[h][:, :1]
        highest = jnp.maximum(before, jnp.max(scores, axis=1, keepdims=True))
        weights = jnp.exp2((scores - highest) * factor)
        shrink = jnp.exp2((before - highest) * factor)
        total = l_s[h][:, :1] * shrink + jnp.sum(weights, axis=1, keepdims=True)
        summed = acc_s[h] * shrink + jnp.dot(
            weights.astype(jnp.bfloat16), block_values, preferred_element_type=jnp.float32
        )
        m_s[h] = jnp.broadcast_to(highest, (rows, width))
        l_s[h] = jnp.broadcast_to(total, (rows, width))
        acc_s[h] = summed

    def each_head(action):
        lax.fori_loop(0, heads, lambda h, c: (action(h), c)[1], 0)

    def when_layer(j, action):
        pl.when((j >= 0) & (j < layers))(lambda: action(j))

    def each_forward(j, h, action):
        slot = j * 2 + side
        action(across(slot, j, h, full))
        action(to_core(slot, slot, h, full))
        pl.when((j > layer) & can_left[2])(lambda: action(column(slot, j, h, full, -2)))
        pl.when((j < layer) & can_right[2])(lambda: action(column(slot, j, h, full, 2)))

    def column_event(j):
        def one(h):
            column(n, j, h, full, 0).wait_recv()
            each_forward(j, h, lambda copy: copy.start())
            attend(j * 2 + side, h)

        each_head(one)

    def side_event(j):
        slot = j * 2 + 1 - side

        def one(h):
            send(n, slot, h, full, side_send.at[j, h], side_recv.at[j, h], {"head": near}).wait_recv()
            to_core(slot, slot, h, full).start()
            attend(slot, h)

        each_head(one)

    def core_event(slot):
        def one(h):
            to_core(n, slot, h, full).wait_recv()
            attend(slot, h)

        each_head(one)

    def at_distance(d, action):
        def one(i, carry):
            when_layer(layer + d * (1 - 2 * i), action)
            return carry

        lax.fori_loop(0, jnp.where(d == 0, 1, 2), one, 0)

    def by_distance(column_action, side_action):
        def one(d, carry):
            at_distance(d, column_action)
            at_distance(d - 1, side_action)
            return carry

        lax.fori_loop(1, layers, one, 0)
        at_distance(jnp.int32(layers - 1), side_action)

    @pl.when(active)
    def _():
        each_head(lambda h: attend(n, h))
        by_distance(column_event, side_event)

    @pl.when(jnp.logical_not(active))
    def _():
        for h in range(heads):
            swap_copy(0, h).wait_recv()
            swap_copy(1, h).wait_recv()
        core_event(seq)
        by_distance(
            lambda j: core_event(j * 2 + side), lambda j: core_event(j * 2 + 1 - side)
        )
        for h in range(heads):
            swap_copy(0, h).wait_send()
            q_v[0, h] = (acc_s[h] / jnp.maximum(l_s[h], 1.0)).astype(jnp.bfloat16)
            swap_copy(2, h).start()

    for h in range(heads):
        @pl.when(active)
        def _():
            att[h, mine] = (acc_s[h] / jnp.maximum(l_s[h], 1.0)).astype(jnp.bfloat16)

        @pl.when(jnp.logical_not(active))
        def _():
            att_in = pltpu.make_async_remote_copy(
                src_ref=q_v.at[0, h], dst_ref=att.at[h, mine],
                send_sem=swap_send.at[2, h], recv_sem=swap_recv.at[2, h],
                device_id={"seq": swap_seq, "head": near}, device_id_type=MESH,
            )
            att_in.wait_recv()

        att_copy(0, h).start()
        att_copy(1, h).start()
        if h > 0:
            att_copy(1, h - 1).wait_recv()
            att_copy(2, h - 1).start()

    own_load.wait()
    for offset in range(1, groups):
        weights_copy(offset).wait_recv()
    result = None
    for h in range(heads):
        if h == heads - 1:
            att_copy(1, h).wait_recv()
            att_copy(2, h).start()
        att_copy(0, h).wait_recv()
        att_copy(2, h).wait_recv()
        joined = jnp.concatenate([att[h, g] for g in range(groups)], axis=1)
        part = jnp.dot(
            joined, wall[h].reshape(groups * width, cols), preferred_element_type=jnp.float32
        )
        result = part if result is None else result + part
    out_ref[...] = result.astype(out_ref.dtype)

    for offset in range(1, groups):
        weights_copy(offset).wait_send()
    for h in range(heads):
        for kind in range(3):
            att_copy(kind, h).wait_send()

    each_own(full, lambda copy: copy.wait_send())

    @pl.when(active)
    def _():
        def column_drain(j):
            each_head(lambda h: each_forward(j, h, lambda copy: copy.wait_send()))

        def side_drain(j):
            slot = j * 2 + 1 - side
            each_head(lambda h: to_core(slot, slot, h, full).wait_send())

        by_distance(column_drain, side_drain)

    @pl.when(jnp.logical_not(active))
    def _():
        for h in range(heads):
            swap_copy(1, h).wait_send()
            swap_copy(2, h).wait_send()


def body(
    tokens, qkv_weight, q_gain, k_gain, out_weight,
    query_cluster, key_cluster, query_slot, key_slot, pairs,
):
    n = lax.axis_size("seq")
    groups = lax.axis_size("head")
    rows, depth = tokens.shape
    heads = pairs.shape[0]
    width = q_gain.shape[0]
    key_clusters = key_slot.shape[1]
    slots = -(-key_clusters // LANES) * LANES
    cols = out_weight.shape[1] // groups

    vmem = pl.BlockSpec(memory_space=pltpu.VMEM)
    smem = pl.BlockSpec(memory_space=pltpu.SMEM)
    anywhere = pl.BlockSpec(memory_space=pl.ANY)
    dma = pltpu.SemaphoreType.DMA
    bf16 = jnp.bfloat16
    return pl.pallas_call(
        functools.partial(kernel, n, groups),
        out_shape=jax.ShapeDtypeStruct((rows, cols), bf16),
        in_specs=[anywhere, anywhere, vmem, vmem, anywhere, vmem, vmem, smem, smem, vmem],
        out_specs=vmem,
        scratch_shapes=[
            pltpu.VMEM((rows, depth), bf16),
            pltpu.VMEM((3, depth, heads * width), bf16),
            pltpu.VMEM((n + 1, heads, 2 * rows + INFO, width), bf16),
            pltpu.VMEM((2, heads, rows, width), bf16),
            pltpu.VMEM((2, heads, rows, slots), bf16),
            pltpu.VMEM((heads, rows, width), jnp.float32),
            pltpu.VMEM((heads, rows, width), jnp.float32),
            pltpu.VMEM((heads, rows, width), jnp.float32),
            pltpu.VMEM((heads, groups, rows, width), bf16),
            pltpu.VMEM((heads, groups, width, cols), bf16),
            dma((5,)),
            dma((n // 2, heads)),
            dma((n // 2, heads)),
            dma((n // 2, heads)),
            dma((n, heads)),
            dma((n // 2, heads)),
            dma((n // 2, heads)),
            dma((n, heads)),
            dma((3, heads)),
            dma((3, heads)),
            dma((3, heads)),
            dma((3, heads)),
            dma((groups,)),
            dma((groups,)),
        ],
        compiler_params=pltpu.CompilerParams(
            collective_id=0, has_side_effects=True, vmem_limit_bytes=56 * 1024 * 1024
        ),
        cost_estimate=pl.CostEstimate(
            flops=2 * rows * depth * 4 * heads * width, bytes_accessed=12 * 1024 * 1024,
            transcendentals=heads * rows * rows * n,
        ),
    )(
        tokens,
        qkv_weight.transpose(1, 0, 2),
        q_gain.reshape(1, width),
        k_gain.reshape(1, width),
        out_weight.reshape(heads, width, out_weight.shape[1]),
        query_cluster.transpose(0, 2, 1),
        key_cluster.transpose(0, 2, 1),
        query_slot,
        key_slot,
        pairs,
    )


def solution(mesh):
    placed = (
        P("seq", None),
        P(None, None, "head"),
        P(),
        P(),
        P("head", None),
        P("head", "seq", None),
        P("head", "seq", None),
        P("head", None),
        P("head", None),
        P("head", None, None),
    )
    return jax.shard_map(
        body, mesh=mesh, in_specs=placed, out_specs=P("seq", "head"), check_vma=False
    )
```

```python
import functools
import math

import jax
import jax.numpy as jnp
from jax import lax
from jax.experimental import pallas as pl
from jax.experimental.pallas import tpu as pltpu
from jax.sharding import PartitionSpec as P

EPSILON = 1e-06
NEG = -2e30
START = -1e30
MESH = pl.DeviceIdType.MESH
LANES = 128
INFO = 16


def normalize(projected, gain):
    mean_square = jnp.mean(projected * projected, axis=-1, keepdims=True)
    return projected * lax.rsqrt(mean_square + EPSILON) * gain


def look_up(labels, table_ref, h):
    found = jnp.zeros(labels.shape, jnp.int32)
    for c in range(table_ref.shape[1]):
        found = jnp.where(labels == c, table_ref[h, c], found)
    return found


def kernel(
    n, groups, tok_ref, wqkv_ref, qg_ref, kg_ref, wout_ref, qc_ref, kc_ref, qslot_ref, kslot_ref,
    pairs_ref, out_ref, tok_v, w_v, kv, q_v, neg_s, m_s, l_s, acc_s, att, wall,
    load_sem, left_send, right_send, side_send, core_send, col_recv, side_recv, core_recv,
    swap_send, swap_recv, att_send, att_recv, wt_send, wt_recv,
):
    heads, rows, width = acc_s.shape
    cols = out_ref.shape[1]
    layers = n // 2
    seq = lax.axis_index("seq")
    mine = lax.axis_index("head")
    layer, side = seq // 2, seq % 2
    active = mine % 2 == layer % 2
    near = mine + 1 - 2 * (mine % 2)
    far = (mine + 2) % groups
    other_layer = layer + 1 - 2 * (layer % 2)
    swap_seq = other_layer * 2 + side
    turn = jnp.where(active, 0, 1)

    tok_load = pltpu.make_async_copy(tok_ref, tok_v, load_sem.at[0])
    tok_load.start()
    w_loads = [pltpu.make_async_copy(wqkv_ref.at[j], w_v.at[j], load_sem.at[1 + j]) for j in range(3)]
    w_loads[1].start()
    own_cols = pl.ds(pl.multiple_of(mine * cols, LANES), cols)
    own_load = pltpu.make_async_copy(wout_ref.at[:, :, own_cols], wall.at[:, mine], load_sem.at[4])
    barrier = pltpu.get_barrier_semaphore()
    met = 1 + groups
    for step in (-2, -1, 1, 2):
        reached = (layer + step >= 0) & (layer + step < layers)
        met = met + jnp.where(reached, 1, 0)

        @pl.when(reached)
        def _():
            pl.semaphore_signal(
                barrier, inc=1, device_id={"seq": seq + 2 * step}, device_id_type=MESH
            )

    pl.semaphore_signal(
        barrier, inc=1, device_id={"seq": layer * 2 + 1 - side}, device_id_type=MESH
    )
    pl.semaphore_signal(
        barrier, inc=1, device_id={"seq": swap_seq, "head": near}, device_id_type=MESH
    )
    for offset in range(1, groups):
        pl.semaphore_signal(
            barrier, inc=1, device_id={"head": (mine + offset) % groups}, device_id_type=MESH
        )

    def send(source, slot, h, part, send_sem, recv_sem, device):
        low, size = part
        return pltpu.make_async_remote_copy(
            src_ref=kv.at[source, h, pl.ds(low, size)], dst_ref=kv.at[slot, h, pl.ds(low, size)],
            send_sem=send_sem, recv_sem=recv_sem, device_id=device, device_id_type=MESH,
        )

    def column(source, j, h, part, step):
        sems = left_send if step < 0 else right_send
        return send(
            source, j * 2 + side, h, part, sems.at[j, h], col_recv.at[j, h],
            {"seq": seq + 2 * step},
        )

    def across(source, j, h, part):
        return send(
            source, j * 2 + side, h, part, side_send.at[j, h], side_recv.at[j, h],
            {"seq": layer * 2 + 1 - side},
        )

    def to_core(source, slot, h, part):
        return send(
            source, slot, h, part, core_send.at[slot, h], core_recv.at[slot, h], {"head": near}
        )

    def swap_copy(kind, h):
        source, target = (
            (q_v.at[0, h], q_v.at[1, h]),
            (neg_s.at[0, h], neg_s.at[1, h]),
            (q_v.at[0, h], att.at[h, near]),
        )[kind]
        return pltpu.make_async_remote_copy(
            src_ref=source, dst_ref=target,
            send_sem=swap_send.at[kind, h], recv_sem=swap_recv.at[kind, h],
            device_id={"seq": swap_seq, "head": near}, device_id_type=MESH,
        )

    full = (0, 2 * rows + INFO)
    key_part = (rows, rows + INFO)
    value_part = (0, rows)

    def weights_copy(offset):
        peer = (mine + offset) % groups
        peer_cols = pl.ds(pl.multiple_of(peer * cols, LANES), cols)
        return pltpu.make_async_remote_copy(
            src_ref=wout_ref.at[:, :, peer_cols], dst_ref=wall.at[:, mine],
            send_sem=wt_send.at[offset], recv_sem=wt_recv.at[offset],
            device_id={"head": peer}, device_id_type=MESH,
        )

    def att_copy(kind, h):
        block = far if kind == 2 else mine
        return pltpu.make_async_remote_copy(
            src_ref=att.at[h, block], dst_ref=att.at[h, block],
            send_sem=att_send.at[kind, h], recv_sem=att_recv.at[kind, h],
            device_id={"head": far if kind == 1 else near}, device_id_type=MESH,
        )

    for h in range(heads):
        placed = look_up(kc_ref[h], kslot_ref, h).astype(jnp.float32)
        lines = [placed[:, r * LANES : (r + 1) * LANES] for r in range(rows // LANES)]
        lines.append(jnp.zeros((INFO - rows // LANES, LANES), jnp.float32))
        kv[n, h, pl.ds(2 * rows, INFO)] = jnp.concatenate(lines, axis=0).astype(jnp.bfloat16)

    tok_load.wait()
    w_loads[1].wait()
    w_loads[2].start()
    w_loads[0].start()
    keys = jnp.dot(tok_v[...], w_v[1], preferred_element_type=jnp.float32)
    for h in range(heads):
        kv[n, h, pl.ds(rows, rows)] = normalize(
            keys[:, h * width : (h + 1) * width], kg_ref[...]
        ).astype(jnp.bfloat16)
    can_left = {step: layer - step >= 0 for step in (1, 2)}
    can_right = {step: layer + step < layers for step in (1, 2)}

    def each_own(part, action):
        for step in (1, 2):
            wanted = active if step == 2 else jnp.logical_not(active)
            for direction, allowed in ((-step, can_left[step]), (step, can_right[step])):

                @pl.when(wanted & allowed)
                def _():
                    for h in range(heads):
                        action(column(n, layer, h, part, direction))

        @pl.when(active)
        def _():
            for h in range(heads):
                action(across(n, layer, h, part))
                action(to_core(n, seq, h, part))

    pl.semaphore_wait(barrier, met)
    each_own(key_part, lambda copy: copy.start())
    w_loads[2].wait()
    values = jnp.dot(tok_v[...], w_v[2], preferred_element_type=jnp.float32)
    for h in range(heads):
        kv[n, h, pl.ds(0, rows)] = values[:, h * width : (h + 1) * width].astype(jnp.bfloat16)

    each_own(value_part, lambda copy: copy.start())
    own_load.start()
    for offset in range(1, groups):
        weights_copy(offset).start()

    w_loads[0].wait()
    queries = jnp.dot(tok_v[...], w_v[0], preferred_element_type=jnp.float32)
    for h in range(heads):
        q_v[0, h] = normalize(queries[:, h * width : (h + 1) * width], qg_ref[...]).astype(
            jnp.bfloat16
        )
    members, lists = pairs_ref.shape[1:]
    slots = neg_s.shape[3]
    padded = -(-members // LANES) * LANES
    member_ids = lax.broadcasted_iota(jnp.int32, (padded, rows), 0)
    slot_ids = lax.broadcasted_iota(jnp.int32, (members, slots), 1)
    for h in range(heads):
        owners = look_up(qc_ref[h], qslot_ref, h)
        owned = jnp.where(member_ids == owners, 1.0, 0.0).T.astype(jnp.bfloat16)
        entries = pairs_ref[h]
        listed = jnp.zeros((members, slots), jnp.float32)
        for k in range(lists):
            listed = jnp.where(entries[:, k : k + 1] == slot_ids, 1.0, listed)
        if padded > members:
            blank = jnp.zeros((padded - members, slots), jnp.float32)
            listed = jnp.concatenate([listed, blank], axis=0)
        allowed = jnp.dot(owned, listed.astype(jnp.bfloat16), preferred_element_type=jnp.float32)
        neg_s[0, h] = jnp.where(allowed > 0.5, 0.0, NEG).astype(jnp.bfloat16)

    @pl.when(jnp.logical_not(active))
    def _():
        for h in range(heads):
            swap_copy(0, h).start()
            swap_copy(1, h).start()

    m_s[...] = jnp.full(m_s.shape, START, jnp.float32)
    l_s[...] = jnp.zeros(l_s.shape, jnp.float32)
    acc_s[...] = jnp.zeros(acc_s.shape, jnp.float32)
    factor = math.log2(math.e) / math.sqrt(width)

    def attend(slot, h):
        block_values = kv[slot, h, pl.ds(0, rows)]
        block_keys = kv[slot, h, pl.ds(rows, rows)]
        info = kv[slot, h, pl.ds(2 * rows, INFO)].astype(jnp.float32)
        row = jnp.concatenate([info[r : r + 1, :] for r in range(rows // LANES)], axis=1)
        ids = lax.broadcasted_iota(jnp.int32, (slots, rows), 0).astype(jnp.float32)
        owner = jnp.where(ids == row, 1.0, 0.0).astype(jnp.bfloat16)
        scores = lax.dot_general(
            q_v[turn, h], block_keys, (((1,), (1,)), ((), ())), preferred_element_type=jnp.float32
        ) + jnp.dot(neg_s[turn, h], owner, preferred_element_type=jnp.float32)
        before = m_s[h][:, :1]
        highest = jnp.maximum(before, jnp.max(scores, axis=1, keepdims=True))
        weights = jnp.exp2((scores - highest) * factor)
        shrink = jnp.exp2((before - highest) * factor)
        total = l_s[h][:, :1] * shrink + jnp.sum(weights, axis=1, keepdims=True)
        summed = acc_s[h] * shrink + jnp.dot(
            weights.astype(jnp.bfloat16), block_values, preferred_element_type=jnp.float32
        )
        m_s[h] = jnp.broadcast_to(highest, (rows, width))
        l_s[h] = jnp.broadcast_to(total, (rows, width))
        acc_s[h] = summed

    def each_head(action):
        lax.fori_loop(0, heads, lambda h, c: (action(h), c)[1], 0)

    def when_layer(j, action):
        pl.when((j >= 0) & (j < layers))(lambda: action(j))

    def each_forward(j, h, action):
        slot = j * 2 + side
        action(across(slot, j, h, full))
        action(to_core(slot, slot, h, full))
        pl.when((j > layer) & can_left[2])(lambda: action(column(slot, j, h, full, -2)))
        pl.when((j < layer) & can_right[2])(lambda: action(column(slot, j, h, full, 2)))

    def column_event(j):
        def one(h):
            column(n, j, h, full, 0).wait_recv()
            each_forward(j, h, lambda copy: copy.start())
            attend(j * 2 + side, h)

        each_head(one)

    def side_piece(j, h):
        slot = j * 2 + 1 - side
        send(n, slot, h, full, side_send.at[j, h], side_recv.at[j, h], {"head": near}).wait_recv()
        to_core(slot, slot, h, full).start()
        attend(slot, h)

    def side_event(j):
        each_head(lambda h: side_piece(j, h))

    def core_piece(slot, h):
        to_core(n, slot, h, full).wait_recv()
        attend(slot, h)

    def core_event(slot):
        each_head(lambda h: core_piece(slot, h))

    farthest = jnp.where(layer * 2 < layers, layers - 1, 0)

    def but_last(action):
        return lambda j: pl.when(j != farthest)(lambda: action(j))

    def share(h):
        att_copy(0, h).start()
        att_copy(1, h).start()
        if h > 0:
            att_copy(1, h - 1).wait_recv()
            att_copy(2, h - 1).start()

    def attended(h):
        return (acc_s[h] / jnp.maximum(l_s[h], 1.0)).astype(jnp.bfloat16)

    def at_distance(d, action):
        def one(i, carry):
            when_layer(layer + d * (1 - 2 * i), action)
            return carry

        lax.fori_loop(0, jnp.where(d == 0, 1, 2), one, 0)

    def by_distance(column_action, side_action):
        def one(d, carry):
            at_distance(d, column_action)
            at_distance(d - 1, side_action)
            return carry

        lax.fori_loop(1, layers, one, 0)
        at_distance(jnp.int32(layers - 1), side_action)

    @pl.when(active)
    def _():
        each_head(lambda h: attend(n, h))
        by_distance(column_event, but_last(side_event))
        for h in range(heads):
            side_piece(farthest, h)
            att[h, mine] = attended(h)
            share(h)

    @pl.when(jnp.logical_not(active))
    def _():
        for h in range(heads):
            swap_copy(0, h).wait_recv()
            swap_copy(1, h).wait_recv()
        core_event(seq)
        by_distance(
            lambda j: core_event(j * 2 + side), but_last(lambda j: core_event(j * 2 + 1 - side))
        )
        for h in range(heads):
            core_piece(farthest * 2 + 1 - side, h)
            swap_copy(0, h).wait_send()
            q_v[0, h] = attended(h)
            swap_copy(2, h).start()
        for h in range(heads):
            returned = pltpu.make_async_remote_copy(
                src_ref=q_v.at[0, h], dst_ref=att.at[h, mine],
                send_sem=swap_send.at[2, h], recv_sem=swap_recv.at[2, h],
                device_id={"seq": swap_seq, "head": near}, device_id_type=MESH,
            )
            returned.wait_recv()
            share(h)

    own_load.wait()
    for offset in range(1, groups):
        weights_copy(offset).wait_recv()
    result = None
    for h in range(heads):
        if h == heads - 1:
            att_copy(1, h).wait_recv()
            att_copy(2, h).start()
        att_copy(0, h).wait_recv()
        att_copy(2, h).wait_recv()
        joined = jnp.concatenate([att[h, g] for g in range(groups)], axis=1)
        part = jnp.dot(
            joined, wall[h].reshape(groups * width, cols), preferred_element_type=jnp.float32
        )
        result = part if result is None else result + part
    out_ref[...] = result.astype(out_ref.dtype)

    for offset in range(1, groups):
        weights_copy(offset).wait_send()
    for h in range(heads):
        for kind in range(3):
            att_copy(kind, h).wait_send()

    each_own(full, lambda copy: copy.wait_send())

    @pl.when(active)
    def _():
        def column_drain(j):
            each_head(lambda h: each_forward(j, h, lambda copy: copy.wait_send()))

        def side_drain(j):
            slot = j * 2 + 1 - side
            each_head(lambda h: to_core(slot, slot, h, full).wait_send())

        by_distance(column_drain, side_drain)

    @pl.when(jnp.logical_not(active))
    def _():
        for h in range(heads):
            swap_copy(1, h).wait_send()
            swap_copy(2, h).wait_send()


def body(
    tokens, qkv_weight, q_gain, k_gain, out_weight,
    query_cluster, key_cluster, query_slot, key_slot, pairs,
):
    n = lax.axis_size("seq")
    groups = lax.axis_size("head")
    rows, depth = tokens.shape
    heads = pairs.shape[0]
    width = q_gain.shape[0]
    key_clusters = key_slot.shape[1]
    slots = -(-key_clusters // LANES) * LANES
    cols = out_weight.shape[1] // groups

    vmem = pl.BlockSpec(memory_space=pltpu.VMEM)
    smem = pl.BlockSpec(memory_space=pltpu.SMEM)
    anywhere = pl.BlockSpec(memory_space=pl.ANY)
    dma = pltpu.SemaphoreType.DMA
    bf16 = jnp.bfloat16
    return pl.pallas_call(
        functools.partial(kernel, n, groups),
        out_shape=jax.ShapeDtypeStruct((rows, cols), bf16),
        in_specs=[anywhere, anywhere, vmem, vmem, anywhere, vmem, vmem, smem, smem, vmem],
        out_specs=vmem,
        scratch_shapes=[
            pltpu.VMEM((rows, depth), bf16),
            pltpu.VMEM((3, depth, heads * width), bf16),
            pltpu.VMEM((n + 1, heads, 2 * rows + INFO, width), bf16),
            pltpu.VMEM((2, heads, rows, width), bf16),
            pltpu.VMEM((2, heads, rows, slots), bf16),
            pltpu.VMEM((heads, rows, width), jnp.float32),
            pltpu.VMEM((heads, rows, width), jnp.float32),
            pltpu.VMEM((heads, rows, width), jnp.float32),
            pltpu.VMEM((heads, groups, rows, width), bf16),
            pltpu.VMEM((heads, groups, width, cols), bf16),
            dma((5,)),
            dma((n // 2, heads)),
            dma((n // 2, heads)),
            dma((n // 2, heads)),
            dma((n, heads)),
            dma((n // 2, heads)),
            dma((n // 2, heads)),
            dma((n, heads)),
            dma((3, heads)),
            dma((3, heads)),
            dma((3, heads)),
            dma((3, heads)),
            dma((groups,)),
            dma((groups,)),
        ],
        compiler_params=pltpu.CompilerParams(
            collective_id=0, has_side_effects=True, vmem_limit_bytes=56 * 1024 * 1024
        ),
        cost_estimate=pl.CostEstimate(
            flops=2 * rows * depth * 4 * heads * width, bytes_accessed=12 * 1024 * 1024,
            transcendentals=heads * rows * rows * n,
        ),
    )(
        tokens,
        qkv_weight.transpose(1, 0, 2),
        q_gain.reshape(1, width),
        k_gain.reshape(1, width),
        out_weight.reshape(heads, width, out_weight.shape[1]),
        query_cluster.transpose(0, 2, 1),
        key_cluster.transpose(0, 2, 1),
        query_slot,
        key_slot,
        pairs,
    )


def solution(mesh):
    placed = (
        P("seq", None),
        P(None, None, "head"),
        P(),
        P(),
        P("head", None),
        P("head", "seq", None),
        P("head", "seq", None),
        P("head", None),
        P("head", None),
        P("head", None, None),
    )
    return jax.shard_map(
        body, mesh=mesh, in_specs=placed, out_specs=P("seq", "head"), check_vma=False
    )
```

```python
import functools
import math

import jax
import jax.numpy as jnp
from jax import lax
from jax.experimental import pallas as pl
from jax.experimental.pallas import tpu as pltpu
from jax.sharding import PartitionSpec as P

EPSILON = 1e-06
NEG = -2e30
START = -1e30
MESH = pl.DeviceIdType.MESH
LANES = 128
INFO = 16


def normalize(projected, gain):
    mean_square = jnp.mean(projected * projected, axis=-1, keepdims=True)
    return projected * lax.rsqrt(mean_square + EPSILON) * gain


def look_up(labels, table_ref, h):
    found = jnp.zeros(labels.shape, jnp.int32)
    for c in range(table_ref.shape[1]):
        found = jnp.where(labels == c, table_ref[h, c], found)
    return found


def kernel(
    n, groups, tok_ref, wqkv_ref, qg_ref, kg_ref, wout_ref, qc_ref, kc_ref, qslot_ref, kslot_ref,
    pairs_ref, out_ref, tok_v, w_v, kv, q_v, neg_s, m_s, l_s, acc_s, att, wall,
    load_sem, left_send, right_send, side_send, core_send, col_recv, side_recv, core_recv,
    swap_send, swap_recv, att_send, att_recv, wt_send, wt_recv,
):
    heads, rows, width = acc_s.shape
    cols = out_ref.shape[1]
    layers = n // 2
    seq = lax.axis_index("seq")
    mine = lax.axis_index("head")
    layer, side = seq // 2, seq % 2
    active = mine % 2 == layer % 2
    near = mine + 1 - 2 * (mine % 2)
    far = (mine + 2) % groups
    other_layer = layer + 1 - 2 * (layer % 2)
    swap_seq = other_layer * 2 + side
    turn = jnp.where(active, 0, 1)

    tok_load = pltpu.make_async_copy(tok_ref, tok_v, load_sem.at[0])
    tok_load.start()
    w_loads = [pltpu.make_async_copy(wqkv_ref.at[j], w_v.at[j], load_sem.at[1 + j]) for j in range(3)]
    w_loads[1].start()
    own_cols = pl.ds(pl.multiple_of(mine * cols, LANES), cols)
    own_load = pltpu.make_async_copy(wout_ref.at[:, :, own_cols], wall.at[:, mine], load_sem.at[4])
    barrier = pltpu.get_barrier_semaphore()
    met = 1 + groups
    for step in (-2, -1, 1, 2):
        reached = (layer + step >= 0) & (layer + step < layers)
        met = met + jnp.where(reached, 1, 0)

        @pl.when(reached)
        def _():
            pl.semaphore_signal(
                barrier, inc=1, device_id={"seq": seq + 2 * step}, device_id_type=MESH
            )

    pl.semaphore_signal(
        barrier, inc=1, device_id={"seq": layer * 2 + 1 - side}, device_id_type=MESH
    )
    pl.semaphore_signal(
        barrier, inc=1, device_id={"seq": swap_seq, "head": near}, device_id_type=MESH
    )
    for offset in range(1, groups):
        pl.semaphore_signal(
            barrier, inc=1, device_id={"head": (mine + offset) % groups}, device_id_type=MESH
        )

    def send(source, slot, h, part, send_sem, recv_sem, device):
        low, size = part
        return pltpu.make_async_remote_copy(
            src_ref=kv.at[source, h, pl.ds(low, size)], dst_ref=kv.at[slot, h, pl.ds(low, size)],
            send_sem=send_sem, recv_sem=recv_sem, device_id=device, device_id_type=MESH,
        )

    def column(source, j, h, part, step):
        sems = left_send if step < 0 else right_send
        return send(
            source, j * 2 + side, h, part, sems.at[j, h], col_recv.at[j, h],
            {"seq": seq + 2 * step},
        )

    def across(source, j, h, part):
        return send(
            source, j * 2 + side, h, part, side_send.at[j, h], side_recv.at[j, h],
            {"seq": layer * 2 + 1 - side},
        )

    def to_core(source, slot, h, part):
        return send(
            source, slot, h, part, core_send.at[slot, h], core_recv.at[slot, h], {"head": near}
        )

    def swap_copy(kind, h):
        source, target = (
            (q_v.at[0, h], q_v.at[1, h]),
            (neg_s.at[0, h], neg_s.at[1, h]),
            (q_v.at[0, h], att.at[h, near]),
        )[kind]
        return pltpu.make_async_remote_copy(
            src_ref=source, dst_ref=target,
            send_sem=swap_send.at[kind, h], recv_sem=swap_recv.at[kind, h],
            device_id={"seq": swap_seq, "head": near}, device_id_type=MESH,
        )

    full = (0, 2 * rows + INFO)
    key_part = (rows, rows + INFO)
    value_part = (0, rows)

    def weights_copy(offset):
        peer = (mine + offset) % groups
        peer_cols = pl.ds(pl.multiple_of(peer * cols, LANES), cols)
        return pltpu.make_async_remote_copy(
            src_ref=wout_ref.at[:, :, peer_cols], dst_ref=wall.at[:, mine],
            send_sem=wt_send.at[offset], recv_sem=wt_recv.at[offset],
            device_id={"head": peer}, device_id_type=MESH,
        )

    def att_copy(kind, h):
        block = far if kind == 2 else mine
        return pltpu.make_async_remote_copy(
            src_ref=att.at[h, block], dst_ref=att.at[h, block],
            send_sem=att_send.at[kind, h], recv_sem=att_recv.at[kind, h],
            device_id={"head": far if kind == 1 else near}, device_id_type=MESH,
        )

    for h in range(heads):
        placed = look_up(kc_ref[h], kslot_ref, h).astype(jnp.float32)
        lines = [placed[:, r * LANES : (r + 1) * LANES] for r in range(rows // LANES)]
        lines.append(jnp.zeros((INFO - rows // LANES, LANES), jnp.float32))
        kv[n, h, pl.ds(2 * rows, INFO)] = jnp.concatenate(lines, axis=0).astype(jnp.bfloat16)

    tok_load.wait()
    w_loads[1].wait()
    w_loads[2].start()
    w_loads[0].start()
    keys = jnp.dot(tok_v[...], w_v[1], preferred_element_type=jnp.float32)
    for h in range(heads):
        kv[n, h, pl.ds(rows, rows)] = normalize(
            keys[:, h * width : (h + 1) * width], kg_ref[...]
        ).astype(jnp.bfloat16)
    can_left = {step: layer - step >= 0 for step in (1, 2)}
    can_right = {step: layer + step < layers for step in (1, 2)}

    def each_own(part, action):
        for step in (1, 2):
            wanted = active if step == 2 else jnp.logical_not(active)
            for direction, allowed in ((-step, can_left[step]), (step, can_right[step])):

                @pl.when(wanted & allowed)
                def _():
                    for h in range(heads):
                        action(column(n, layer, h, part, direction))

        @pl.when(active)
        def _():
            for h in range(heads):
                action(across(n, layer, h, part))
                action(to_core(n, seq, h, part))

    pl.semaphore_wait(barrier, met)
    each_own(key_part, lambda copy: copy.start())
    for offset in range(1, groups):
        weights_copy(offset).start()
    w_loads[2].wait()
    values = jnp.dot(tok_v[...], w_v[2], preferred_element_type=jnp.float32)
    for h in range(heads):
        kv[n, h, pl.ds(0, rows)] = values[:, h * width : (h + 1) * width].astype(jnp.bfloat16)

    each_own(value_part, lambda copy: copy.start())
    own_load.start()

    w_loads[0].wait()
    queries = jnp.dot(tok_v[...], w_v[0], preferred_element_type=jnp.float32)
    for h in range(heads):
        q_v[0, h] = normalize(queries[:, h * width : (h + 1) * width], qg_ref[...]).astype(
            jnp.bfloat16
        )
    members, lists = pairs_ref.shape[1:]
    slots = neg_s.shape[3]
    padded = -(-members // LANES) * LANES
    member_ids = lax.broadcasted_iota(jnp.int32, (padded, rows), 0)
    slot_ids = lax.broadcasted_iota(jnp.int32, (members, slots), 1)
    for h in range(heads):
        owners = look_up(qc_ref[h], qslot_ref, h)
        owned = jnp.where(member_ids == owners, 1.0, 0.0).T.astype(jnp.bfloat16)
        entries = pairs_ref[h]
        listed = jnp.zeros((members, slots), jnp.float32)
        for k in range(lists):
            listed = jnp.where(entries[:, k : k + 1] == slot_ids, 1.0, listed)
        if padded > members:
            blank = jnp.zeros((padded - members, slots), jnp.float32)
            listed = jnp.concatenate([listed, blank], axis=0)
        allowed = jnp.dot(owned, listed.astype(jnp.bfloat16), preferred_element_type=jnp.float32)
        neg_s[0, h] = jnp.where(allowed > 0.5, 0.0, NEG).astype(jnp.bfloat16)

    @pl.when(jnp.logical_not(active))
    def _():
        for h in range(heads):
            swap_copy(0, h).start()
            swap_copy(1, h).start()

    m_s[...] = jnp.full(m_s.shape, START, jnp.float32)
    l_s[...] = jnp.zeros(l_s.shape, jnp.float32)
    acc_s[...] = jnp.zeros(acc_s.shape, jnp.float32)
    factor = math.log2(math.e) / math.sqrt(width)

    def attend(slot, h):
        block_values = kv[slot, h, pl.ds(0, rows)]
        block_keys = kv[slot, h, pl.ds(rows, rows)]
        info = kv[slot, h, pl.ds(2 * rows, INFO)].astype(jnp.float32)
        row = jnp.concatenate([info[r : r + 1, :] for r in range(rows // LANES)], axis=1)
        ids = lax.broadcasted_iota(jnp.int32, (slots, rows), 0).astype(jnp.float32)
        owner = jnp.where(ids == row, 1.0, 0.0).astype(jnp.bfloat16)
        scores = lax.dot_general(
            q_v[turn, h], block_keys, (((1,), (1,)), ((), ())), preferred_element_type=jnp.float32
        ) + jnp.dot(neg_s[turn, h], owner, preferred_element_type=jnp.float32)
        before = m_s[h][:, :1]
        highest = jnp.maximum(before, jnp.max(scores, axis=1, keepdims=True))
        weights = jnp.exp2((scores - highest) * factor)
        shrink = jnp.exp2((before - highest) * factor)
        total = l_s[h][:, :1] * shrink + jnp.sum(weights, axis=1, keepdims=True)
        summed = acc_s[h] * shrink + jnp.dot(
            weights.astype(jnp.bfloat16), block_values, preferred_element_type=jnp.float32
        )
        m_s[h] = jnp.broadcast_to(highest, (rows, width))
        l_s[h] = jnp.broadcast_to(total, (rows, width))
        acc_s[h] = summed

    def each_head(action):
        lax.fori_loop(0, heads, lambda h, c: (action(h), c)[1], 0)

    def when_layer(j, action):
        pl.when((j >= 0) & (j < layers))(lambda: action(j))

    def each_forward(j, h, action):
        slot = j * 2 + side
        pl.when((j > layer) & can_left[2])(lambda: action(column(slot, j, h, full, -2)))
        pl.when((j < layer) & can_right[2])(lambda: action(column(slot, j, h, full, 2)))
        action(across(slot, j, h, full))
        action(to_core(slot, slot, h, full))

    def column_event(j):
        def one(h):
            column(n, j, h, full, 0).wait_recv()
            each_forward(j, h, lambda copy: copy.start())
            attend(j * 2 + side, h)

        each_head(one)

    def side_event(j):
        slot = j * 2 + 1 - side

        def one(h):
            send(n, slot, h, full, side_send.at[j, h], side_recv.at[j, h], {"head": near}).wait_recv()
            to_core(slot, slot, h, full).start()
            attend(slot, h)

        each_head(one)

    def core_event(slot):
        def one(h):
            to_core(n, slot, h, full).wait_recv()
            attend(slot, h)

        each_head(one)

    def at_distance(d, action):
        def one(i, carry):
            when_layer(layer + d * (1 - 2 * i), action)
            return carry

        lax.fori_loop(0, jnp.where(d == 0, 1, 2), one, 0)

    def by_distance(column_action, side_action):
        def one(d, carry):
            at_distance(d, column_action)
            at_distance(d - 1, side_action)
            return carry

        lax.fori_loop(1, layers, one, 0)
        at_distance(jnp.int32(layers - 1), side_action)

    @pl.when(active)
    def _():
        each_head(lambda h: attend(n, h))
        by_distance(column_event, side_event)

    @pl.when(jnp.logical_not(active))
    def _():
        for h in range(heads):
            swap_copy(0, h).wait_recv()
            swap_copy(1, h).wait_recv()
        core_event(seq)
        by_distance(
            lambda j: core_event(j * 2 + side), lambda j: core_event(j * 2 + 1 - side)
        )
        for h in range(heads):
            swap_copy(0, h).wait_send()
            q_v[0, h] = (acc_s[h] / jnp.maximum(l_s[h], 1.0)).astype(jnp.bfloat16)
            swap_copy(2, h).start()

    for h in range(heads):
        @pl.when(active)
        def _():
            att[h, mine] = (acc_s[h] / jnp.maximum(l_s[h], 1.0)).astype(jnp.bfloat16)

        @pl.when(jnp.logical_not(active))
        def _():
            att_in = pltpu.make_async_remote_copy(
                src_ref=q_v.at[0, h], dst_ref=att.at[h, mine],
                send_sem=swap_send.at[2, h], recv_sem=swap_recv.at[2, h],
                device_id={"seq": swap_seq, "head": near}, device_id_type=MESH,
            )
            att_in.wait_recv()

        att_copy(0, h).start()
        att_copy(1, h).start()
        if h > 0:
            att_copy(1, h - 1).wait_recv()
            att_copy(2, h - 1).start()

    own_load.wait()
    for offset in range(1, groups):
        weights_copy(offset).wait_recv()
    result = None
    for h in range(heads):
        if h == heads - 1:
            att_copy(1, h).wait_recv()
            att_copy(2, h).start()
        att_copy(0, h).wait_recv()
        att_copy(2, h).wait_recv()
        joined = jnp.concatenate([att[h, g] for g in range(groups)], axis=1)
        part = jnp.dot(
            joined, wall[h].reshape(groups * width, cols), preferred_element_type=jnp.float32
        )
        result = part if result is None else result + part
    out_ref[...] = result.astype(out_ref.dtype)

    for offset in range(1, groups):
        weights_copy(offset).wait_send()
    for h in range(heads):
        for kind in range(3):
            att_copy(kind, h).wait_send()

    each_own(full, lambda copy: copy.wait_send())

    @pl.when(active)
    def _():
        def column_drain(j):
            each_head(lambda h: each_forward(j, h, lambda copy: copy.wait_send()))

        def side_drain(j):
            slot = j * 2 + 1 - side
            each_head(lambda h: to_core(slot, slot, h, full).wait_send())

        by_distance(column_drain, side_drain)

    @pl.when(jnp.logical_not(active))
    def _():
        for h in range(heads):
            swap_copy(1, h).wait_send()
            swap_copy(2, h).wait_send()


def body(
    tokens, qkv_weight, q_gain, k_gain, out_weight,
    query_cluster, key_cluster, query_slot, key_slot, pairs,
):
    n = lax.axis_size("seq")
    groups = lax.axis_size("head")
    rows, depth = tokens.shape
    heads = pairs.shape[0]
    width = q_gain.shape[0]
    key_clusters = key_slot.shape[1]
    slots = -(-key_clusters // LANES) * LANES
    cols = out_weight.shape[1] // groups

    vmem = pl.BlockSpec(memory_space=pltpu.VMEM)
    smem = pl.BlockSpec(memory_space=pltpu.SMEM)
    anywhere = pl.BlockSpec(memory_space=pl.ANY)
    dma = pltpu.SemaphoreType.DMA
    bf16 = jnp.bfloat16
    return pl.pallas_call(
        functools.partial(kernel, n, groups),
        out_shape=jax.ShapeDtypeStruct((rows, cols), bf16),
        in_specs=[anywhere, anywhere, vmem, vmem, anywhere, vmem, vmem, smem, smem, vmem],
        out_specs=vmem,
        scratch_shapes=[
            pltpu.VMEM((rows, depth), bf16),
            pltpu.VMEM((3, depth, heads * width), bf16),
            pltpu.VMEM((n + 1, heads, 2 * rows + INFO, width), bf16),
            pltpu.VMEM((2, heads, rows, width), bf16),
            pltpu.VMEM((2, heads, rows, slots), bf16),
            pltpu.VMEM((heads, rows, width), jnp.float32),
            pltpu.VMEM((heads, rows, width), jnp.float32),
            pltpu.VMEM((heads, rows, width), jnp.float32),
            pltpu.VMEM((heads, groups, rows, width), bf16),
            pltpu.VMEM((heads, groups, width, cols), bf16),
            dma((5,)),
            dma((n // 2, heads)),
            dma((n // 2, heads)),
            dma((n // 2, heads)),
            dma((n, heads)),
            dma((n // 2, heads)),
            dma((n // 2, heads)),
            dma((n, heads)),
            dma((3, heads)),
            dma((3, heads)),
            dma((3, heads)),
            dma((3, heads)),
            dma((groups,)),
            dma((groups,)),
        ],
        compiler_params=pltpu.CompilerParams(
            collective_id=0, has_side_effects=True, vmem_limit_bytes=56 * 1024 * 1024
        ),
        cost_estimate=pl.CostEstimate(
            flops=2 * rows * depth * 4 * heads * width, bytes_accessed=12 * 1024 * 1024,
            transcendentals=heads * rows * rows * n,
        ),
    )(
        tokens,
        qkv_weight.transpose(1, 0, 2),
        q_gain.reshape(1, width),
        k_gain.reshape(1, width),
        out_weight.reshape(heads, width, out_weight.shape[1]),
        query_cluster.transpose(0, 2, 1),
        key_cluster.transpose(0, 2, 1),
        query_slot,
        key_slot,
        pairs,
    )


def solution(mesh):
    placed = (
        P("seq", None),
        P(None, None, "head"),
        P(),
        P(),
        P("head", None),
        P("head", "seq", None),
        P("head", "seq", None),
        P("head", None),
        P("head", None),
        P("head", None, None),
    )
    return jax.shard_map(
        body, mesh=mesh, in_specs=placed, out_specs=P("seq", "head"), check_vma=False
    )
```
